256 devices in a mesh: ctx: 32 (over x, y, core), tp: 8 (over z).
Axes of the slice: x: 4, y: 4, z: 8, core: 2. Of those that a mesh axis runs over, the one named last changes fastest.
Arguments:
- x_first: bfloat16 [32, 8192], P(None, 'ctx')
- x_second: bfloat16 [32, 8192], P(None, 'ctx')
- norm_gain: bfloat16 [8192], P('ctx'), may hold values from 0.099609375 to 1.8984375
- w_query: bfloat16 [8192, 8192], P('ctx', 'tp')
- key_value_weight: bfloat16 [8192, 2048], P('ctx', 'tp')
- w_out: bfloat16 [8192, 8192], P('tp', 'ctx'), may hold values from -0.125 to 0.125
- key_cache: bfloat16 [1376, 128, 1024], P('ctx', None, 'tp')
- value_cache: bfloat16 [1376, 128, 1024], P('ctx', None, 'tp'), may hold values from -12 to 12
- lengths: int32 [32], replicated, may hold values from 128 to 16384, as said below
- page_table: int32 [32, 128], replicated, may hold values from -1 to 1375, as said below
- move_from: int32 [64], replicated, may hold values from 0 to 1375, as said below
- move_to: int32 [64], replicated, may hold values from 0 to 1375, as said below
Outputs:
- out_first: bfloat16 [32, 8192], P('tp', 'ctx')
- out_second: bfloat16 [32, 8192], P('tp', 'ctx')
- moved_k: bfloat16 [1376, 128, 1024], P('ctx', None, 'tp')
- moved_v: bfloat16 [1376, 128, 1024], P('ctx', None, 'tp')
The draws below stay inside these ranges and needn't reach their ends.
Inputs may be any that keep to these rules, and one draw needn't show every extreme that they name: `lengths`: one request has exactly 16384 cached tokens; every other has fewer than 8192. `page_table`: entry (r, p) is shard * 43 + slot for p < ceil(lengths[r] / 128) and -1 after; no global slot appears twice; the pages of a shard fill its slots from 0 upwards and stay below slot 35, which some shard fills completely. `move_from`: entries 2 * c to 2 * c + 1 are distinct slots of shard c that appear in page_table. `move_to`: distinct slots, each at or above slot 35 of its shard; the 2 pages that one shard gives up go to 2 different shards; a receiving shard gets exactly 8 pages.
All inputs are finite; a program needn't handle non-finite values.
Results may differ from the reference program's by a relative error of at most 0.018.
Values may be sent and summed in bfloat16 or wider, within the bound.
A program may use at most 64 MiB of HBM per device.

```python
import jax
import jax.numpy as jnp
from jax import lax

MODEL_WIDTH = 8192
QUERY_HEADS = 64
KEY_VALUE_HEADS = 8
HEAD_SIZE = 128
PAGE_TOKENS = 128
REQUEST_PAGES = 128
MIG_DEV = 2
REQ = 32
LOAD_CAP = 35
SHARD_SLOTS = 43
N_CTX = 32


def layout(key):
    key_pair, key_token, key_long, key_target = jax.random.split(key, 4)
    half_pages = REQUEST_PAGES // 2
    fewest = REQUEST_PAGES // 32
    pair_pages = jax.random.randint(key_pair, (REQ // 2,), fewest, half_pages - fewest + 1)
    request_ids = jnp.arange(REQ, dtype=jnp.int32)
    longest = jax.random.randint(key_long, (), 0, REQ)
    partner = jnp.bitwise_xor(longest, 1)
    paired = jnp.where(request_ids % 2 == 0, pair_pages[request_ids // 2], half_pages - pair_pages[request_ids // 2])
    page_count = jnp.where(request_ids == longest, REQUEST_PAGES, jnp.where(request_ids == partner, half_pages // 2, paired)).astype(jnp.int32)
    token_part = jax.random.randint(key_token, (REQ,), 1, PAGE_TOKENS + 1)
    all_lengths = jnp.where(request_ids == longest, PAGE_TOKENS * REQUEST_PAGES, (page_count - 1) * PAGE_TOKENS + token_part).astype(jnp.int32)
    first_page = (jnp.cumsum(page_count) - page_count).astype(jnp.int32)
    page_ids = jnp.arange(REQUEST_PAGES, dtype=jnp.int32)
    counter = (first_page[:, None] + page_ids[None, :]).reshape(-1)
    is_used = (page_ids[None, :] < page_count[:, None]).reshape(-1)
    shard_of = counter % N_CTX
    slot_rank = counter // N_CTX
    flat_table = jnp.where(is_used, shard_of * SHARD_SLOTS + slot_rank, -1).astype(jnp.int32)
    onehot = ((shard_of[:, None] == jnp.arange(N_CTX)[None, :]) & is_used[:, None]).astype(jnp.int32)
    page_score = jnp.where(is_used, jnp.repeat(all_lengths, REQUEST_PAGES) * (REQ * REQUEST_PAGES) + jnp.arange(REQ * REQUEST_PAGES, dtype=jnp.int32), -1)
    shard_scores = jnp.where(onehot.T > 0, page_score[None, :], -1)
    unused_values, chosen = lax.top_k(shard_scores, MIG_DEV)
    sources = flat_table[chosen.reshape(-1)].astype(jnp.int32)
    target_count = N_CTX // 4
    others = jax.random.permutation(key_target, N_CTX - 1)[:target_count - 1]
    targets = jnp.concatenate([others, jnp.array([N_CTX - 1], dtype=others.dtype)]).astype(jnp.int32)
    moved_index = jnp.arange(MIG_DEV * N_CTX, dtype=jnp.int32)
    target_slots = (targets[moved_index % target_count] * SHARD_SLOTS + LOAD_CAP + moved_index // target_count).astype(jnp.int32)
    return (all_lengths, flat_table.reshape(REQ, REQUEST_PAGES), sources, target_slots)


def draw_lengths(key, part):
    return layout(key)[0]


def draw_page_table(key, part):
    return layout(key)[1]


def draw_move_from(key, part):
    return layout(key)[2]


def draw_move_to(key, part):
    return layout(key)[3]


def shared_projection(key):
    return jax.random.normal(key, (MODEL_WIDTH, KEY_VALUE_HEADS, HEAD_SIZE), jnp.float32) * MODEL_WIDTH ** (-0.5)


def draw_w_query(key, part):
    common = shared_projection(key)
    key = jax.random.fold_in(key, 53)
    group_size = QUERY_HEADS // KEY_VALUE_HEADS
    noise = jax.random.normal(key, (MODEL_WIDTH, KEY_VALUE_HEADS, group_size, HEAD_SIZE), jnp.float32) * MODEL_WIDTH ** (-0.5)
    weight_rows = 0.75 * common[:, :, None, :] + 0.66 * noise
    return weight_rows.reshape(MODEL_WIDTH, QUERY_HEADS * HEAD_SIZE).astype(jnp.bfloat16)


def draw_key_value_weight(key, part):
    common = shared_projection(key)
    key = jax.random.fold_in(key, 59)
    value_part = jax.random.normal(key, (MODEL_WIDTH, KEY_VALUE_HEADS, HEAD_SIZE), jnp.float32) * MODEL_WIDTH ** (-0.5)
    weight_rows = jnp.stack([common, value_part], axis=2)
    return weight_rows.reshape(MODEL_WIDTH, 2 * KEY_VALUE_HEADS * HEAD_SIZE).astype(jnp.bfloat16)


def draw_x_first(key, part):
    key = jax.random.fold_in(key, 11)
    key_value = jax.random.fold_in(key, 0)
    rising = 0.6 + 1.2 * jnp.arange(MODEL_WIDTH, dtype=jnp.float32) / MODEL_WIDTH
    value_rows = jax.random.normal(key_value, (REQ, MODEL_WIDTH), jnp.float32) * rising[None, :]
    return value_rows.astype(jnp.bfloat16)


def draw_x_second(key, part):
    key = jax.random.fold_in(key, 23)
    key_value = jax.random.fold_in(key, 0)
    rising = 0.6 + 1.2 * jnp.arange(MODEL_WIDTH, dtype=jnp.float32) / MODEL_WIDTH
    value_rows = jax.random.normal(key_value, (REQ, MODEL_WIDTH), jnp.float32) * rising[None, :]
    return value_rows.astype(jnp.bfloat16)


def draw_key_cache(key, part):
    key = jax.random.fold_in(key, 37)
    key_value = jax.random.fold_in(key, 0)
    slot_total = N_CTX * SHARD_SLOTS
    array_shape = (slot_total, PAGE_TOKENS, KEY_VALUE_HEADS, HEAD_SIZE)
    value_rows = 0.7 * jax.random.normal(key_value, array_shape, jnp.float32)
    return value_rows.reshape(slot_total, PAGE_TOKENS, KEY_VALUE_HEADS * HEAD_SIZE).astype(jnp.bfloat16)


def draw_value_cache(key, part):
    key = jax.random.fold_in(key, 41)
    key_level, key_noise = jax.random.split(key)
    width = KEY_VALUE_HEADS * HEAD_SIZE
    slot_total = N_CTX * SHARD_SLOTS
    level = 2.0 * jax.random.normal(key_level, (slot_total, 1, width), jnp.float32)
    noise = jax.random.normal(key_noise, (slot_total, PAGE_TOKENS, width), jnp.float32)
    return jnp.clip(level + noise, -12.0, 12.0).astype(jnp.bfloat16)


def shard_levels(stream_key, extent, shards, smallest, top_value):
    factor_of, own = 1.0, jax.random.fold_in(stream_key, 6)
    for axis_at, parts in shards:
        steps = jnp.exp(jax.random.uniform(jax.random.fold_in(own, axis_at), (parts,), jnp.float32, smallest / len(shards), top_value / len(shards)))
        factor_of = factor_of * jnp.repeat(steps, extent[axis_at] // parts).reshape([-1 if axis == axis_at else 1 for axis in range(len(extent))])
    return factor_of


def normal_values(own_key, extent, scale, bound, pieces=(), held_as=jnp.bfloat16):
    factor_of = shard_levels(own_key, extent, pieces, -0.22, 0.18) if pieces else 1.0
    result = jax.random.normal(own_key, extent, jnp.float32) * scale * factor_of
    return jnp.minimum(jnp.maximum(result, -bound), bound).astype(held_as)


def setup_inputs(seed: int = 0) -> dict:
    key_list = jax.random.split(jax.random.key(seed), 13)
    x_first = draw_x_first(jax.random.fold_in(key_list[12], 71), 0)
    x_second = draw_x_second(jax.random.fold_in(key_list[12], 71), 0)
    norm_gain = jnp.clip(1.0 + 0.18 * jax.random.normal(key_list[2], (MODEL_WIDTH,), jnp.float32), 0.099609375, 1.8984375).astype(jnp.bfloat16)
    w_query = draw_w_query(jax.random.fold_in(key_list[12], 71), 0)
    key_value_weight = draw_key_value_weight(jax.random.fold_in(key_list[12], 71), 0)
    w_out = normal_values(key_list[5], (QUERY_HEADS * HEAD_SIZE, MODEL_WIDTH), (QUERY_HEADS * HEAD_SIZE // 4) ** -0.5, 0.125, ((0, 8), (1, 32)))
    key_cache = draw_key_cache(jax.random.fold_in(key_list[12], 71), 0)
    value_cache = draw_value_cache(jax.random.fold_in(key_list[12], 71), 0)
    lengths = draw_lengths(jax.random.fold_in(key_list[12], 71), 0)
    page_table = draw_page_table(jax.random.fold_in(key_list[12], 71), 0)
    move_from = draw_move_from(jax.random.fold_in(key_list[12], 71), 0)
    move_to = draw_move_to(jax.random.fold_in(key_list[12], 71), 0)
    return dict(x_first=x_first, x_second=x_second, norm_gain=norm_gain, w_query=w_query, key_value_weight=key_value_weight, w_out=w_out, key_cache=key_cache, value_cache=value_cache, lengths=lengths, page_table=page_table, move_from=move_from, move_to=move_to)


THETA = 500000.0
EPSILON = 1e-05
NEGATIVE = -1e+30

def rotate(vectors, positions):
    half_dim = HEAD_SIZE // 2
    inverse = THETA ** (-(jnp.arange(half_dim, dtype=jnp.float32) * 2.0 / HEAD_SIZE))
    angles = positions.astype(jnp.float32)[:, None] * inverse[None, :]
    cosine = jnp.cos(angles)[:, None, :]
    sine_part = jnp.sin(angles)[:, None, :]
    first_half = vectors[..., :half_dim]
    second_half = vectors[..., half_dim:]
    return jnp.concatenate([first_half * cosine - second_half * sine_part, second_half * cosine + first_half * sine_part], axis=-1)

def project(inputs, norm_gain, w_query, key_value_weight, positions):
    widened = inputs.astype(jnp.float32)
    squares = lax.optimization_barrier(jnp.sum(widened * widened, axis=1))
    inverse_root_mean = lax.rsqrt(squares / MODEL_WIDTH + EPSILON)
    scaled = (widened * norm_gain.astype(jnp.float32)[None, :]).astype(jnp.bfloat16)
    query_raw = jnp.dot(scaled, w_query, preferred_element_type=jnp.float32) * inverse_root_mean[:, None]
    key_value_unrotated = jnp.dot(scaled, key_value_weight, preferred_element_type=jnp.float32) * inverse_root_mean[:, None]
    count_of_rows = inputs.shape[0]
    queries = rotate(query_raw.reshape(count_of_rows, QUERY_HEADS, HEAD_SIZE), positions).astype(jnp.bfloat16)
    key_value_pair = key_value_unrotated.reshape(count_of_rows, KEY_VALUE_HEADS, 2, HEAD_SIZE)
    new_keys = rotate(key_value_pair[:, :, 0], positions).astype(jnp.bfloat16)
    new_values = key_value_pair[:, :, 1].astype(jnp.bfloat16)
    return (queries, new_keys, new_values)

def attend(queries, new_keys, new_values, page_table, lengths, key_cache, value_cache):
    query_group_size = QUERY_HEADS // KEY_VALUE_HEADS
    score_scale = HEAD_SIZE ** (-0.5)
    offsets = jnp.arange(REQUEST_PAGES, dtype=jnp.int32)[:, None] * PAGE_TOKENS + jnp.arange(PAGE_TOKENS, dtype=jnp.int32)[None, :]

    def one_request(request_items):
        query_vector, keys_new, values_new, page_ids, length = request_items
        clamped_pages = jnp.maximum(page_ids, 0)
        keys_of_page = key_cache[clamped_pages].reshape(REQUEST_PAGES, PAGE_TOKENS, KEY_VALUE_HEADS, HEAD_SIZE).astype(jnp.float32)
        values_of_page = value_cache[clamped_pages].reshape(REQUEST_PAGES, PAGE_TOKENS, KEY_VALUE_HEADS, HEAD_SIZE).astype(jnp.float32)
        grouped_queries = query_vector.reshape(KEY_VALUE_HEADS, query_group_size, HEAD_SIZE).astype(jnp.float32)
        scores = jnp.einsum('kgd,bpkd->kgbp', grouped_queries, keys_of_page) * score_scale
        is_valid = (offsets < length) & (page_ids[:, None] >= 0)
        scores = jnp.where(is_valid, scores, NEGATIVE)
        block_max = lax.optimization_barrier(jnp.max(scores, axis=-1))
        weights = jnp.where(is_valid, jnp.exp(scores - block_max[..., None]), 0.0).astype(jnp.bfloat16)
        weights = lax.optimization_barrier(weights).astype(jnp.float32)
        block_total = lax.optimization_barrier(jnp.sum(weights, axis=-1))
        block_out = jnp.einsum('kgbp,bpkd->kgbd', weights, values_of_page)
        own_scores = jnp.einsum('kgd,nkd->kgn', grouped_queries, keys_new.astype(jnp.float32)) * score_scale
        own_max = lax.optimization_barrier(jnp.max(own_scores, axis=-1))
        own_weights = jnp.exp(own_scores - own_max[..., None]).astype(jnp.bfloat16)
        own_weights = lax.optimization_barrier(own_weights).astype(jnp.float32)
        own_total = lax.optimization_barrier(jnp.sum(own_weights, axis=-1))
        own_out = jnp.einsum('kgn,nkd->kgd', own_weights, values_new.astype(jnp.float32))
        peak_score = jnp.maximum(lax.optimization_barrier(jnp.max(block_max, axis=-1)), own_max)
        block_scale = jnp.exp(block_max - peak_score[..., None])
        own_scale = jnp.exp(own_max - peak_score)
        numerator = lax.optimization_barrier(jnp.sum(block_scale[..., None] * block_out, axis=2)) + own_scale[..., None] * own_out
        denominator = lax.optimization_barrier(jnp.sum(block_scale * block_total, axis=-1)) + own_scale * own_total
        return (numerator / denominator[..., None]).reshape(QUERY_HEADS * HEAD_SIZE).astype(jnp.bfloat16)
    return lax.map(one_request, (queries, new_keys, new_values, page_table, lengths))

def finish(inputs, attention, w_out):
    return (inputs.astype(jnp.float32) + jnp.dot(attention, w_out, preferred_element_type=jnp.float32)).astype(jnp.bfloat16)

def relocate(cache, move_from, move_to):
    moved_pages = cache[move_from]
    cleared = cache.at[move_from].set(jnp.zeros_like(moved_pages))
    return cleared.at[move_to].set(moved_pages)

def retable(page_table, move_from, move_to):
    matches = page_table[:, :, None] == move_from[None, None, :]
    target = lax.optimization_barrier(jnp.sum(jnp.where(matches, move_to[None, None, :], 0), axis=-1)).astype(jnp.int32)
    return jnp.where(jnp.any(matches, axis=-1), target, page_table).astype(jnp.int32)

def reference(x_first, x_second, norm_gain, w_query, key_value_weight, w_out, key_cache, value_cache, lengths, page_table, move_from, move_to):
    first_query, first_key, first_value = project(x_first, norm_gain, w_query, key_value_weight, lengths)
    first_attention = attend(first_query, first_key[:, None], first_value[:, None], page_table, lengths, key_cache, value_cache)
    out_first = finish(x_first, first_attention, w_out)
    moved_k = relocate(key_cache, move_from, move_to)
    moved_v = relocate(value_cache, move_from, move_to)
    table_after = retable(page_table, move_from, move_to)
    second_query, second_key, second_value = project(x_second, norm_gain, w_query, key_value_weight, lengths + 1)
    keys_both = jnp.stack([first_key, second_key], axis=1)
    values_both = jnp.stack([first_value, second_value], axis=1)
    second_attention = attend(second_query, keys_both, values_both, table_after, lengths, moved_k, moved_v)
    out_second = finish(x_second, second_attention, w_out)
    return (out_first, out_second, moved_k, moved_v)
```

```python
import functools

import jax
import jax.numpy as jnp
import numpy as np
from jax import lax
from jax.experimental import pallas as pl
from jax.experimental.pallas import tpu as pltpu
from jax.sharding import PartitionSpec as P

HEAD = 128
GROUP = 8
PAGE = 128
ARRIVALS = 8
THETA = 500000.0
EPSILON = 1e-05
NEGATIVE = -1e30
SCALE = HEAD**-0.5
MESH = pl.DeviceIdType.MESH
F32 = jnp.float32
BF16 = jnp.bfloat16

TURN_HIGH = 6.28125
TURN_MID = float(np.float32(np.round((2 * np.pi - TURN_HIGH) * 2.0**20) / 2.0**20))
TURN_LOW = float(np.float32(2 * np.pi - TURN_HIGH - TURN_MID))


def turn_reduced(angle):
    turns = jnp.floor(angle * (1.0 / (2 * np.pi)) + 0.5)
    return ((angle - turns * TURN_HIGH) - turns * TURN_MID) - turns * TURN_LOW


def split2(v):
    high = v.astype(BF16).astype(F32)
    return high, v - high


def split3(v):
    high, rest = split2(v)
    mid, low = split2(rest)
    return high, mid, low


def kernel(
    n,
    tsize,
    grid_xyc,
    width,
    lengths_s,
    from_s,
    to_v,
    table_v,
    inverse_v,
    x1_v,
    x2_v,
    gain_v,
    wq_hbm,
    wkv_hbm,
    wo_hbm,
    kc_hbm,
    vc_hbm,
    o1_v,
    o2_v,
    mk_hbm,
    mv_hbm,
    wq,
    wkv,
    wo,
    kbuf,
    vbuf,
    asm,
    send_a,
    recv_a,
    q_all,
    own_kv,
    slots_t,
    tab_v,
    tab_s,
    blocks,
    scan,
    send_c,
    recv_c,
    att_all,
    att_f,
    p_send,
    p_recv,
    kxy,
    vxy,
    sib_send,
    sib_recv,
    load_sem,
    out_sem,
    tab_sem,
    send_sem,
    recv_sem,
):
    nx, ny, nc = grid_xyc
    me = lax.axis_index("ctx")
    mt = lax.axis_index("tp")
    core = lax.rem(me, nc)
    yi = lax.rem(me // nc, ny)
    xi = me // (nc * ny)
    requests = x1_v.shape[0]
    pages = table_v.shape[1]
    slots = kbuf.shape[0]
    cap = slots - ARRIVALS
    rows_t = requests // tsize

    loads = [
        pltpu.make_async_copy(src, dst, load_sem.at[i])
        for i, (src, dst) in enumerate(
            [(wq_hbm, wq), (wkv_hbm, wkv), (kc_hbm, kbuf), (vc_hbm, vbuf), (wo_hbm, wo)]
        )
    ]
    for copy in loads:
        copy.start()

    barrier = pltpu.get_barrier_semaphore()

    def greet_ctx(j, _):
        pl.semaphore_signal(
            barrier, inc=1, device_id={"ctx": lax.rem(me + j, n)}, device_id_type=MESH
        )
        return 0

    lax.fori_loop(1, n, greet_ctx, 0)

    def greet_tp(j, _):
        pl.semaphore_signal(
            barrier, inc=1, device_id={"tp": lax.rem(mt + j, tsize)}, device_id_type=MESH
        )
        return 0

    lax.fori_loop(1, tsize, greet_tp, 0)

    def remote(src, dst, at, axis, peer):
        return pltpu.make_async_remote_copy(
            src_ref=src,
            dst_ref=dst,
            send_sem=send_sem.at[at],
            recv_sem=recv_sem.at[at],
            device_id={axis: peer},
            device_id_type=MESH,
        )

    def wait_bytes(ref, sem):
        pltpu.make_async_copy(ref, ref, sem).wait()

    x_both = jnp.concatenate([x1_v[...], x2_v[...]], axis=0).astype(F32)
    squares = jnp.sum(x_both * x_both, axis=1, keepdims=True)
    scaled = (x_both * gain_v[...].astype(F32)).astype(BF16)
    sq_high, sq_low = split2(jnp.broadcast_to(squares, (2 * requests, HEAD)))
    loads[0].wait()
    loads[1].wait()
    for step in range(2):
        rows = slice(step * requests, (step + 1) * requests)
        asm[pl.ds(20 + step, requests, stride=32), :] = sq_high[rows]
        asm[pl.ds(22 + step, requests, stride=32), :] = sq_low[rows]
    kv_part = jnp.dot(scaled, wkv[...], preferred_element_type=F32)
    for step in range(2):
        rows = slice(step * requests, (step + 1) * requests)
        asm[pl.ds(16 + step, requests, stride=32), :] = kv_part[rows, :HEAD]
        asm[pl.ds(18 + step, requests, stride=32), :] = kv_part[rows, HEAD:]
    for h in range(GROUP):
        part = jnp.dot(scaled, wq[:, h * HEAD : (h + 1) * HEAD], preferred_element_type=F32)
        for step in range(2):
            rows = slice(step * requests, (step + 1) * requests)
            asm[pl.ds(step * GROUP + h, requests, stride=32), :] = part[rows]

    pl.semaphore_wait(barrier, n - 1 + tsize - 1)

    def send_partial(j, _):
        peer = lax.rem(me + j, n)
        send_a[peer] = asm[pl.ds(pl.multiple_of(peer * 32, 32), 32), :].astype(BF16)
        remote(send_a.at[peer], recv_a.at[j], 0, "ctx", peer).start()
        return 0

    lax.fori_loop(1, n, send_partial, 0)

    loads[2].wait()
    loads[3].wait()
    for i in range(2):
        leaving = jnp.clip(from_s[2 * me + i] - me * slots, 0, slots - 1)
        kxy[yi, xi, i] = kbuf[leaving]
        vxy[xi, yi, i] = vbuf[leaving]
    for d in range(1, nx):
        peer = (lax.rem(xi + d, nx) * ny + yi) * nc + core
        remote(kxy.at[yi, xi], kxy.at[yi, xi], 5, "ctx", peer).start()
    for d in range(1, ny):
        peer = (xi * ny + lax.rem(yi + d, ny)) * nc + core
        remote(vxy.at[xi, yi], vxy.at[xi, yi], 6, "ctx", peer).start()

    local_table = table_v[...] - me * slots
    code = (
        lax.broadcasted_iota(jnp.int32, (requests, pages), 0) * pages
        + lax.broadcasted_iota(jnp.int32, (requests, pages), 1)
        + 1
    )
    slots_t[...] = jnp.zeros(slots_t.shape, jnp.int32)
    for s in range(cap):
        found = jnp.where(local_table == s, code, 0)
        slots_t[s : s + 1, :] = jnp.max(found, axis=0, keepdims=True)
    by_slot = slots_t[...]
    rows_n = tab_v.shape[0]
    code_col = jnp.max(by_slot[:rows_n], axis=1, keepdims=True)
    code_row = jnp.max(by_slot.T, axis=0, keepdims=True)
    owner_col = jnp.right_shift(code_col - 1, pages.bit_length() - 1)
    owner_row = jnp.right_shift(code_row - 1, pages.bit_length() - 1)
    wide = (rows_n, 128)
    row_id = lax.broadcasted_iota(jnp.int32, wide, 0)
    lane_id = lax.broadcasted_iota(jnp.int32, wide, 1)
    earlier = (owner_col == owner_row) & (lane_id < row_id) & (code_row > 0)
    prev_col = jnp.max(jnp.where(earlier, lane_id + 1, 0), axis=1, keepdims=True)
    held = (owner_row == row_id) & (code_row > 0)
    last_col = jnp.max(jnp.where(held, lane_id + 1, 0), axis=1, keepdims=True)
    targets = to_v[...] - cap
    moves = targets.shape[1]
    move_row = lax.broadcasted_iota(jnp.int32, (rows_n, moves), 0)
    move_lane = lax.broadcasted_iota(jnp.int32, (rows_n, moves), 1)
    sibling = me + 1 - 2 * core
    arrive_col = jnp.max(
        jnp.where(targets - me * slots == move_row, move_lane + 1, 0), axis=1, keepdims=True
    )
    arrive_sib = jnp.max(
        jnp.where(targets - sibling * slots == move_row, move_lane + 1, 0), axis=1, keepdims=True
    )
    packed = jnp.zeros(wide, jnp.int32)
    for i, column in enumerate([code_col, prev_col, last_col, arrive_col, arrive_sib]):
        packed = jnp.where(lane_id == i, column, packed)
    tab_v[...] = packed
    tab_copy = pltpu.make_async_copy(tab_v, tab_s, tab_sem)
    tab_copy.start()

    position = lengths_s[me].astype(F32)
    inverse = inverse_v[...]
    lane = lax.broadcasted_iota(jnp.int32, (1, HEAD), 1)
    sign = jnp.where(lane < HEAD // 2, -1.0, 1.0)
    angles = jnp.concatenate([position * inverse, (position + 1.0) * inverse], axis=0)
    angles = turn_reduced(angles)
    cosine = jnp.cos(angles)
    sine = jnp.sin(angles) * sign

    def by_step(v, count):
        return jnp.concatenate(
            [jnp.broadcast_to(v[0:1], (count, HEAD)), jnp.broadcast_to(v[1:2], (count, HEAD))],
            axis=0,
        )

    tab_copy.wait()
    total = asm[pl.ds(pl.multiple_of(me * 32, 32), 32), :]
    wait_bytes(recv_a.at[pl.ds(1, n - 1)], recv_sem.at[0])
    for j in range(1, n):
        total = total + recv_a[j].astype(F32)
    square = total[20:22] + total[22:24]
    rms = lax.rsqrt(square / width + EPSILON)

    def rotated(v, count):
        return v * by_step(cosine, count) + pltpu.roll(v, HEAD // 2, 1) * by_step(sine, count)

    q_own = rotated(total[:16] * by_step(rms, GROUP), GROUP).astype(BF16)
    q_all[me] = q_own

    def send_query(j, _):
        peer = lax.rem(me + j, n)
        remote(q_all.at[me], q_all.at[me], 1, "ctx", peer).start()
        return 0

    lax.fori_loop(1, n, send_query, 0)

    wait_bytes(kxy.at[0, pl.ds(0, nx - 1)], recv_sem.at[5])
    wait_bytes(vxy.at[0, pl.ds(0, ny - 1)], recv_sem.at[6])
    for d in range(1, ny):
        peer = (xi * ny + lax.rem(yi + d, ny)) * nc + core
        remote(kxy.at[yi], kxy.at[yi], 7, "ctx", peer).start()
    for d in range(1, nx):
        peer = (lax.rem(xi + d, nx) * ny + yi) * nc + core
        remote(vxy.at[xi], vxy.at[xi], 8, "ctx", peer).start()

    new_k = rotated(total[16:18] * rms, 1).astype(BF16).astype(F32)
    new_v = (total[18:20] * rms).astype(BF16).astype(F32)
    qf = q_own.astype(F32)
    second = lax.broadcasted_iota(jnp.int32, (16, HEAD), 0) >= GROUP
    own_1 = jnp.sum(qf * new_k[0:1], axis=1, keepdims=True) * SCALE
    own_2 = jnp.sum(qf * new_k[1:2], axis=1, keepdims=True) * SCALE
    own_1 = jnp.broadcast_to(own_1, (16, HEAD))
    own_2 = jnp.where(second, jnp.broadcast_to(own_2, (16, HEAD)), NEGATIVE)
    own_max = jnp.maximum(own_1, own_2)
    own_w1 = jnp.exp(own_1 - own_max).astype(BF16).astype(F32)
    own_w2 = jnp.exp(own_2 - own_max).astype(BF16).astype(F32)
    own_total = own_w1 + own_w2
    own_out = own_w1 * new_v[0:1] + own_w2 * new_v[1:2]
    own_kv[0] = own_max
    own_kv[1] = own_total
    own_kv[2] = own_out

    scan[0, 0:16] = jnp.full((16, HEAD), NEGATIVE, F32)
    scan[0, 16:48] = jnp.zeros((32, HEAD), F32)
    wait_bytes(q_all.at[pl.ds(0, n - 1)], recv_sem.at[1])
    token = lax.broadcasted_iota(jnp.int32, (16, PAGE), 1)
    per = 7 if cap % 7 == 0 else 1

    def page_block(b, _):
        for i in range(per):
            s = b * per + i
            flat = jnp.maximum(tab_s[s, 0] - 1, 0)
            present = tab_s[s, 0] > 0
            owner = jnp.right_shift(flat, pages.bit_length() - 1)
            page = jnp.bitwise_and(flat, pages - 1)
            count = jnp.where(present, lengths_s[owner] - page * PAGE, 0)
            scores = lax.dot_general(
                q_all[owner], kbuf[s], (((1,), (1,)), ((), ())), preferred_element_type=F32
            )
            valid = token < count
            scores = jnp.where(valid, scores * SCALE, NEGATIVE)
            top = jnp.max(scores, axis=1, keepdims=True)
            weights = jnp.where(valid, jnp.exp(scores - top), 0.0).astype(BF16)
            amount = jnp.sum(weights.astype(F32), axis=1, keepdims=True)
            out = jnp.dot(weights, vbuf[s], preferred_element_type=F32)
            blocks[i, 0:16] = jnp.broadcast_to(top, (16, HEAD))
            blocks[i, 16:32] = jnp.broadcast_to(amount, (16, HEAD))
            blocks[i, 32:48] = out
        for i in range(per):
            s = b * per + i
            before = tab_s[s, 1]
            top_b, top = scan[before, 0:16], blocks[i, 0:16]
            peak = jnp.maximum(top_b, top)
            scale_b, scale = jnp.exp(top_b - peak), jnp.exp(top - peak)
            scan[s + 1, 0:16] = peak
            scan[s + 1, 16:32] = scan[before, 16:32] * scale_b + blocks[i, 16:32] * scale
            scan[s + 1, 32:48] = scan[before, 32:48] * scale_b + blocks[i, 32:48] * scale
        return 0

    lax.fori_loop(0, cap // per, page_block, 0)

    lane16 = lax.broadcasted_iota(jnp.int32, (16, HEAD), 1)

    def message(r):
        at = tab_s[r, 2]
        t3 = split3(scan[at, 0:16])
        a2 = split2(scan[at, 16:32])
        small = jnp.zeros((16, HEAD), F32)
        for i, part in enumerate(t3 + a2):
            small = jnp.where(lane16 == i, part, small)
        return scan[at, 32:48].astype(BF16), small.astype(BF16)

    def send_blocks(j, _):
        peer = lax.rem(me + j, n)
        big, small = message(peer)
        send_c[peer, 0:16] = big
        send_c[peer, 16:32] = small
        remote(send_c.at[peer], recv_c.at[j], 2, "ctx", peer).start()
        return 0

    lax.fori_loop(1, n, send_blocks, 0)
    big, small = message(me)
    recv_c[0, 0:16] = big
    recv_c[0, 16:32] = small

    leave_0 = from_s[2 * me] - me * slots
    leave_1 = from_s[2 * me + 1] - me * slots

    def clear(s, _):
        gone = (s == leave_0) | (s == leave_1)
        kbuf[s] = jnp.where(gone, jnp.zeros((), BF16), kbuf[s])
        vbuf[s] = jnp.where(gone, jnp.zeros((), BF16), vbuf[s])
        return 0

    lax.fori_loop(0, cap, clear, 0)

    pick = lax.broadcasted_iota(jnp.int32, (HEAD, 2 * HEAD), 0)
    half = lax.broadcasted_iota(jnp.int32, (HEAD, 2 * HEAD), 1) >= HEAD
    chooser = jnp.where(
        half, jnp.where((pick == 3) | (pick == 4), 1.0, 0.0), jnp.where(pick < 3, 1.0, 0.0)
    ).astype(BF16)
    wait_bytes(recv_c.at[pl.ds(1, n - 1)], recv_sem.at[2])
    spread = jnp.dot(
        recv_c[:, 16:32].reshape(n * 16, HEAD), chooser, preferred_element_type=F32
    )
    for j in range(n):
        asm[j * 32 : j * 32 + 16, :] = spread[j * 16 : j * 16 + 16, :HEAD]
        asm[j * 32 + 16 : j * 32 + 32, :] = spread[j * 16 : j * 16 + 16, HEAD:]
    peak = own_kv[0]
    for j in range(n):
        peak = jnp.maximum(peak, asm[j * 32 : j * 32 + 16, :])
    own_scale = jnp.exp(own_kv[0] - peak)
    denominator = own_kv[1] * own_scale
    numerator = own_kv[2] * own_scale
    for j in range(n):
        scale = jnp.exp(asm[j * 32 : j * 32 + 16, :] - peak)
        denominator = denominator + asm[j * 32 + 16 : j * 32 + 32, :] * scale
        numerator = numerator + recv_c[j, 0:16].astype(F32) * scale
    att_all[me] = (numerator / denominator).astype(BF16)

    def send_attention(j, _):
        peer = lax.rem(me + j, n)
        remote(att_all.at[me], att_all.at[me], 3, "ctx", peer).start()
        return 0

    lax.fori_loop(1, n, send_attention, 0)

    wait_bytes(kxy.at[pl.ds(0, ny - 1)], recv_sem.at[7])
    wait_bytes(vxy.at[pl.ds(0, nx - 1)], recv_sem.at[8])

    def source_of(mark):
        index = jnp.maximum(mark - 1, 0)
        device = jnp.right_shift(index, 1)
        which = jnp.bitwise_and(index, 1)
        src_core = lax.rem(device, nc)
        src_y = lax.rem(device // nc, ny)
        src_x = device // (nc * ny)
        return src_x, src_y, src_core, which

    for i in range(ARRIVALS):
        src_x, src_y, _, which = source_of(tab_s[i, 4])
        sib_send[0, i] = kxy[src_y, src_x, which]
        sib_send[1, i] = vxy[src_x, src_y, which]
    remote(sib_send, sib_recv, 9, "ctx", sibling).start()

    loads[4].wait()
    wait_bytes(att_all.at[pl.ds(0, n - 1)], recv_sem.at[3])
    for r in range(requests):
        att_f[r * 16 : r * 16 + 16, :] = att_all[r].astype(F32)
    attention = jnp.concatenate(
        [
            jnp.concatenate(
                [att_f[pl.ds(step * GROUP + h, requests, stride=16), :] for h in range(GROUP)],
                axis=1,
            )
            for step in range(2)
        ],
        axis=0,
    ).astype(BF16)
    projected = jnp.dot(attention, wo[...], preferred_element_type=F32)
    for t in range(tsize):
        for step in range(2):
            p_send[t, step * rows_t : (step + 1) * rows_t] = projected[
                step * requests + t * rows_t : step * requests + (t + 1) * rows_t
            ]

    def send_projected(j, _):
        peer = lax.rem(mt + j, tsize)
        remote(p_send.at[peer], p_recv.at[j], 4, "tp", peer).start()
        return 0

    lax.fori_loop(1, tsize, send_projected, 0)

    wait_bytes(sib_recv, recv_sem.at[9])
    for i in range(ARRIVALS):
        mark = tab_s[i, 3]
        src_x, src_y, src_core, which = source_of(mark)
        here = src_core == core
        arrived = mark > 0
        new_page = jnp.where(here, kxy[src_y, src_x, which], sib_recv[0, i])
        kbuf[cap + i] = jnp.where(arrived, new_page, kbuf[cap + i])
        new_page = jnp.where(here, vxy[src_x, src_y, which], sib_recv[1, i])
        vbuf[cap + i] = jnp.where(arrived, new_page, vbuf[cap + i])
    out_k = pltpu.make_async_copy(kbuf, mk_hbm, out_sem.at[0])
    out_v = pltpu.make_async_copy(vbuf, mv_hbm, out_sem.at[1])
    out_k.start()
    out_v.start()

    residual_1 = jnp.zeros((rows_t, x1_v.shape[1]), F32)
    residual_2 = residual_1
    x1_f, x2_f = x1_v[...].astype(F32), x2_v[...].astype(F32)
    for t in range(tsize):
        rows = slice(t * rows_t, (t + 1) * rows_t)
        residual_1 = jnp.where(mt == t, x1_f[rows], residual_1)
        residual_2 = jnp.where(mt == t, x2_f[rows], residual_2)

    wait_bytes(p_recv.at[pl.ds(1, tsize - 1)], recv_sem.at[4])
    summed = p_send[mt]
    for j in range(1, tsize):
        summed = summed + p_recv[j]
    o1_v[...] = (residual_1 + summed[:rows_t]).astype(BF16)
    o2_v[...] = (residual_2 + summed[rows_t:]).astype(BF16)

    wait_bytes(recv_a.at[pl.ds(1, n - 1)], send_sem.at[0])
    wait_bytes(q_all.at[pl.ds(0, n - 1)], send_sem.at[1])
    wait_bytes(recv_c.at[pl.ds(1, n - 1)], send_sem.at[2])
    wait_bytes(att_all.at[pl.ds(0, n - 1)], send_sem.at[3])
    wait_bytes(p_recv.at[pl.ds(1, tsize - 1)], send_sem.at[4])
    wait_bytes(kxy.at[0, pl.ds(0, nx - 1)], send_sem.at[5])
    wait_bytes(vxy.at[0, pl.ds(0, ny - 1)], send_sem.at[6])
    wait_bytes(kxy.at[pl.ds(0, ny - 1)], send_sem.at[7])
    wait_bytes(vxy.at[pl.ds(0, nx - 1)], send_sem.at[8])
    wait_bytes(sib_send, send_sem.at[9])
    out_k.wait()
    out_v.wait()


def grid_of(n):
    cores = 2
    side = int(round((n // cores) ** 0.5))
    return (n // cores // side, side, cores)


def per_device(
    n,
    tsize,
    x_first,
    x_second,
    norm_gain,
    w_query,
    key_value_weight,
    w_out,
    key_cache,
    value_cache,
    lengths,
    page_table,
    move_from,
    move_to,
):
    requests, depth = x_first.shape
    slots = key_cache.shape[0]
    cap = slots - ARRIVALS
    nx, ny, nc = grid_of(n)
    rows_t = requests // tsize
    half = HEAD // 2
    inverse = THETA ** (-(np.arange(half, dtype=np.float64) * 2.0 / HEAD))
    inverse = np.concatenate([inverse, inverse])[None, :].astype(np.float32)
    rows_n = -(-max(cap, requests) // 8) * 8
    vmem = pl.BlockSpec(memory_space=pltpu.VMEM)
    smem = pl.BlockSpec(memory_space=pltpu.SMEM)
    anywhere = pl.BlockSpec(memory_space=pl.ANY)
    out = pl.pallas_call(
        functools.partial(kernel, n, tsize, (nx, ny, nc), depth * n),
        out_shape=(
            jax.ShapeDtypeStruct((rows_t, depth), BF16),
            jax.ShapeDtypeStruct((rows_t, depth), BF16),
            jax.ShapeDtypeStruct(key_cache.shape, BF16),
            jax.ShapeDtypeStruct(value_cache.shape, BF16),
        ),
        in_specs=[smem, smem] + [vmem] * 6 + [anywhere] * 5,
        out_specs=(vmem, vmem, anywhere, anywhere),
        scratch_shapes=[
            pltpu.VMEM(w_query.shape, BF16),
            pltpu.VMEM(key_value_weight.shape, BF16),
            pltpu.VMEM(w_out.shape, BF16),
            pltpu.VMEM(key_cache.shape, BF16),
            pltpu.VMEM(value_cache.shape, BF16),
            pltpu.VMEM((n * 32, HEAD), F32),
            pltpu.VMEM((n, 32, HEAD), BF16),
            pltpu.VMEM((n, 32, HEAD), BF16),
            pltpu.VMEM((n, 16, HEAD), BF16),
            pltpu.VMEM((3, 16, HEAD), F32),
            pltpu.VMEM((128, page_table.shape[1]), jnp.int32),
            pltpu.VMEM((rows_n, 128), jnp.int32),
            pltpu.SMEM((rows_n, 128), jnp.int32),
            pltpu.VMEM((8, 48, HEAD), F32),
            pltpu.VMEM((cap + 1, 48, HEAD), F32),
            pltpu.VMEM((n, 32, HEAD), BF16),
            pltpu.VMEM((n, 32, HEAD), BF16),
            pltpu.VMEM((n, 16, HEAD), BF16),
            pltpu.VMEM((n * 16, HEAD), F32),
            pltpu.VMEM((tsize, 2 * rows_t, depth), F32),
            pltpu.VMEM((tsize, 2 * rows_t, depth), F32),
            pltpu.VMEM((ny, nx, 2, PAGE, HEAD), BF16),
            pltpu.VMEM((nx, ny, 2, PAGE, HEAD), BF16),
            pltpu.VMEM((2, ARRIVALS, PAGE, HEAD), BF16),
            pltpu.VMEM((2, ARRIVALS, PAGE, HEAD), BF16),
            pltpu.SemaphoreType.DMA((5,)),
            pltpu.SemaphoreType.DMA((2,)),
            pltpu.SemaphoreType.DMA,
            pltpu.SemaphoreType.DMA((10,)),
            pltpu.SemaphoreType.DMA((10,)),
        ],
        compiler_params=pltpu.CompilerParams(
            collective_id=0, has_side_effects=True, vmem_limit_bytes=40 * 1024 * 1024
        ),
        name="decode_two_steps",
    )(
        lengths,
        move_from,
        move_to.reshape(1, -1),
        page_table,
        jnp.asarray(inverse),
        x_first,
        x_second,
        norm_gain.reshape(1, -1),
        w_query,
        key_value_weight,
        w_out,
        key_cache,
        value_cache,
    )
    return out


def solution(mesh):
    n, tsize = mesh.shape["ctx"], mesh.shape["tp"]
    in_specs = (
        P(None, "ctx"),
        P(None, "ctx"),
        P("ctx"),
        P("ctx", "tp"),
        P("ctx", "tp"),
        P("tp", "ctx"),
        P("ctx", None, "tp"),
        P("ctx", None, "tp"),
        P(),
        P(),
        P(),
        P(),
    )
    out_specs = (P("tp", "ctx"), P("tp", "ctx"), P("ctx", None, "tp"), P("ctx", None, "tp"))
    return jax.shard_map(
        functools.partial(per_device, n, tsize),
        mesh=mesh,
        in_specs=in_specs,
        out_specs=out_specs,
        check_vma=False,
    )
```

```python
import functools

import jax
import jax.numpy as jnp
import numpy as np
from jax import lax
from jax.experimental import pallas as pl
from jax.experimental.pallas import tpu as pltpu
from jax.sharding import PartitionSpec as P

HEAD = 128
GROUP = 8
PAGE = 128
ARRIVALS = 8
THETA = 500000.0
EPSILON = 1e-05
NEGATIVE = -1e30
SCALE = HEAD**-0.5
MESH = pl.DeviceIdType.MESH
F32 = jnp.float32
BF16 = jnp.bfloat16
VMEM_GRANT = 58 * 1024 * 1024
AFTER_QUERY, AFTER_BLOCKS = 2, 1
CHUNKS = 4

TURN_HIGH = 6.28125
TURN_MID = float(np.float32(np.round((2 * np.pi - TURN_HIGH) * 2.0**20) / 2.0**20))
TURN_LOW = float(np.float32(2 * np.pi - TURN_HIGH - TURN_MID))


def turn_reduced(angle):
    turns = jnp.floor(angle * (1.0 / (2 * np.pi)) + 0.5)
    return ((angle - turns * TURN_HIGH) - turns * TURN_MID) - turns * TURN_LOW


def split2(v):
    high = v.astype(BF16).astype(F32)
    return high, v - high


def kernel(
    n,
    tsize,
    grid_xyc,
    width,
    lengths_hbm,
    from_hbm,
    to_hbm,
    table_hbm,
    x1_hbm,
    x2_hbm,
    gain_hbm,
    wq_hbm,
    wkv_hbm,
    wo_hbm,
    kc_hbm,
    vc_hbm,
    o1_v,
    o2_v,
    mk_hbm,
    mv_hbm,
    lengths_s,
    from_s,
    to_v,
    table_v,
    x1_v,
    x2_v,
    gain_v,
    wq,
    wkv,
    wo,
    kbuf,
    vbuf,
    asm,
    send_a,
    recv_a,
    q_all,
    own_kv,
    slots_t,
    tab_v,
    tab_s,
    scores,
    weights,
    blocks,
    scan,
    send_c,
    recv_c,
    send_m,
    recv_m,
    att_all,
    att_f,
    p_send,
    p_recv,
    kxy,
    vxy,
    sib_send,
    sib_recv,
    load_sem,
    out_sem,
    tab_sem,
    send_sem,
    recv_sem,
):
    nx, ny, nc = grid_xyc
    me = lax.axis_index("ctx")
    mt = lax.axis_index("tp")
    core = lax.rem(me, nc)
    yi = lax.rem(me // nc, ny)
    xi = me // (nc * ny)
    requests = x1_v.shape[0]
    pages = table_v.shape[1]
    slots = kbuf.shape[0]
    cap = slots - ARRIVALS
    rows_t = requests // tsize

    loads = [
        pltpu.make_async_copy(src, dst, load_sem.at[i])
        for i, (src, dst) in enumerate(
            [
                (wq_hbm, wq),
                (wkv_hbm, wkv),
                (kc_hbm, kbuf),
                (vc_hbm, vbuf),
                (wo_hbm, wo),
                (x1_hbm, x1_v),
                (x2_hbm, x2_v),
                (gain_hbm, gain_v),
                (lengths_hbm, lengths_s),
                (from_hbm, from_s),
                (to_hbm, to_v.at[0]),
                (table_hbm, table_v),
            ]
        )
    ]
    for at in (5, 6, 7, 1, 0, 2, 3, 8, 9, 10, 11, 4):
        loads[at].start()

    def hops(d, size):
        return min(d, size - d)

    offsets = [(a, b, c) for a in range(nx) for b in range(ny) for c in range(nc)][1:]
    offsets.sort(key=lambda o: -(hops(o[0], nx) + hops(o[1], ny)))
    peers = [
        (
            (lax.rem(xi + a, nx) * ny + lax.rem(yi + b, ny)) * nc + lax.rem(core + c, nc),
            (a * ny + b) * nc + c,
        )
        for a, b, c in offsets
    ]

    def far_first(size):
        return sorted(range(1, size), key=lambda d: -hops(d, size))

    barrier = pltpu.get_barrier_semaphore()

    for peer, _ in peers:
        pl.semaphore_signal(barrier, inc=1, device_id={"ctx": peer}, device_id_type=MESH)
    for j in far_first(tsize):
        pl.semaphore_signal(
            barrier, inc=1, device_id={"tp": lax.rem(mt + j, tsize)}, device_id_type=MESH
        )

    def remote(src, dst, at, axis, peer):
        return pltpu.make_async_remote_copy(
            src_ref=src,
            dst_ref=dst,
            send_sem=send_sem.at[at],
            recv_sem=recv_sem.at[at],
            device_id={axis: peer},
            device_id_type=MESH,
        )

    def wait_bytes(ref, sem):
        pltpu.make_async_copy(ref, ref, sem).wait()

    for at in (5, 6, 7):
        loads[at].wait()
    x_both = jnp.concatenate([x1_v[...], x2_v[...]], axis=0).astype(F32)
    squares = jnp.sum(x_both * x_both, axis=1, keepdims=True)
    scaled = (x_both * gain_v[...].astype(F32)[None, :]).astype(BF16)
    sq_high, sq_low = split2(jnp.broadcast_to(squares, (2 * requests, HEAD)))
    loads[0].wait()
    loads[1].wait()
    for step in range(2):
        rows = slice(step * requests, (step + 1) * requests)
        asm[pl.ds(20 + step, requests, stride=32), :] = sq_high[rows]
        asm[pl.ds(22 + step, requests, stride=32), :] = sq_low[rows]
    kv_part = jnp.dot(scaled, wkv[...], preferred_element_type=F32)
    for step in range(2):
        rows = slice(step * requests, (step + 1) * requests)
        asm[pl.ds(16 + step, requests, stride=32), :] = kv_part[rows, :HEAD]
        asm[pl.ds(18 + step, requests, stride=32), :] = kv_part[rows, HEAD:]
    for h in range(GROUP):
        part = jnp.dot(scaled, wq[:, h * HEAD : (h + 1) * HEAD], preferred_element_type=F32)
        for step in range(2):
            rows = slice(step * requests, (step + 1) * requests)
            asm[pl.ds(step * GROUP + h, requests, stride=32), :] = part[rows]

    for r in range(requests):
        send_a[r] = asm[r * 32 : r * 32 + 32, :].astype(BF16)
    pl.semaphore_wait(barrier, n - 1 + tsize - 1)

    for peer, at in peers:
        remote(send_a.at[peer], recv_a.at[at], 0, "ctx", peer).start()

    for at in (2, 3, 8, 9, 10, 11):
        loads[at].wait()
    for i in range(2):
        leaving = jnp.clip(from_s[2 * me + i] - me * slots, 0, slots - 1)
        kxy[yi, xi, i] = kbuf[leaving]
        vxy[xi, yi, i] = vbuf[leaving]
    for d in far_first(nx):
        peer = (lax.rem(xi + d, nx) * ny + yi) * nc + core
        remote(kxy.at[yi, xi], kxy.at[yi, xi], 5, "ctx", peer).start()
    for d in far_first(ny):
        peer = (xi * ny + lax.rem(yi + d, ny)) * nc + core
        remote(vxy.at[xi, yi], vxy.at[xi, yi], 6, "ctx", peer).start()

    local_table = table_v[...] - me * slots
    code = (
        lax.broadcasted_iota(jnp.int32, (requests, pages), 0) * pages
        + lax.broadcasted_iota(jnp.int32, (requests, pages), 1)
        + 1
    )
    slots_t[...] = jnp.zeros(slots_t.shape, jnp.int32)
    for s in range(cap):
        found = jnp.where(local_table == s, code, 0)
        slots_t[s : s + 1, :] = jnp.max(found, axis=0, keepdims=True)
    by_slot = slots_t[...]
    rows_n = tab_v.shape[0]
    code_col = jnp.max(by_slot[:rows_n], axis=1, keepdims=True)
    code_row = jnp.max(by_slot.T, axis=0, keepdims=True)
    owner_col = jnp.right_shift(code_col - 1, pages.bit_length() - 1)
    owner_row = jnp.right_shift(code_row - 1, pages.bit_length() - 1)
    wide = (rows_n, 128)
    row_id = lax.broadcasted_iota(jnp.int32, wide, 0)
    lane_id = lax.broadcasted_iota(jnp.int32, wide, 1)
    earlier = (owner_col == owner_row) & (lane_id < row_id) & (code_row > 0)
    prev_col = jnp.max(jnp.where(earlier, lane_id + 1, 0), axis=1, keepdims=True)
    held = (owner_row == row_id) & (code_row > 0)
    last_col = jnp.max(jnp.where(held, lane_id + 1, 0), axis=1, keepdims=True)
    targets = to_v[...] - cap
    moves = targets.shape[1]
    move_row = lax.broadcasted_iota(jnp.int32, (rows_n, moves), 0)
    move_lane = lax.broadcasted_iota(jnp.int32, (rows_n, moves), 1)
    sibling = me + 1 - 2 * core
    arrive_col = jnp.max(
        jnp.where(targets - me * slots == move_row, move_lane + 1, 0), axis=1, keepdims=True
    )
    arrive_sib = jnp.max(
        jnp.where(targets - sibling * slots == move_row, move_lane + 1, 0), axis=1, keepdims=True
    )
    packed = jnp.zeros(wide, jnp.int32)
    for i, column in enumerate([code_col, prev_col, last_col, arrive_col, arrive_sib]):
        packed = jnp.where(lane_id == i, column, packed)
    tab_v[...] = packed
    tab_copy = pltpu.make_async_copy(tab_v, tab_s, tab_sem)
    tab_copy.start()

    position = lengths_s[me].astype(F32)
    lane = lax.broadcasted_iota(jnp.int32, (1, HEAD), 1)
    inverse = jnp.zeros((1, HEAD), F32)
    for i in range(HEAD // 2):
        rate = float(np.float32(THETA ** (-2.0 * i / HEAD)))
        inverse = jnp.where(lane % (HEAD // 2) == i, rate, inverse)
    sign = jnp.where(lane < HEAD // 2, -1.0, 1.0)
    angles = jnp.concatenate([position * inverse, (position + 1.0) * inverse], axis=0)
    angles = turn_reduced(angles)
    cosine = jnp.cos(angles)
    sine = jnp.sin(angles) * sign

    def by_step(v, count):
        return jnp.concatenate(
            [jnp.broadcast_to(v[0:1], (count, HEAD)), jnp.broadcast_to(v[1:2], (count, HEAD))],
            axis=0,
        )

    tab_copy.wait()
    total = asm[pl.ds(pl.multiple_of(me * 32, 32), 32), :]
    wait_bytes(recv_a.at[pl.ds(1, n - 1)], recv_sem.at[0])
    for j in range(1, n):
        total = total + recv_a[j].astype(F32)
    square = total[20:22] + total[22:24]
    rms = lax.rsqrt(square / width + EPSILON)

    def rotated(v, count):
        return v * by_step(cosine, count) + pltpu.roll(v, HEAD // 2, 1) * by_step(sine, count)

    q_own = rotated(total[:16] * by_step(rms, GROUP), GROUP).astype(BF16)
    q_all[me] = q_own

    for peer, _ in peers:
        remote(q_all.at[me], q_all.at[me], 1, "ctx", peer).start()

    wait_bytes(kxy.at[0, pl.ds(0, nx - 1)], recv_sem.at[5])
    wait_bytes(vxy.at[0, pl.ds(0, ny - 1)], recv_sem.at[6])

    def second_hop(first, last):
        for part in range(first, min(last, nx)):
            for d in far_first(ny):
                peer = (xi * ny + lax.rem(yi + d, ny)) * nc + core
                remote(kxy.at[yi, part], kxy.at[yi, part], 7, "ctx", peer).start()
        for part in range(first, min(last, ny)):
            for d in far_first(nx):
                peer = (lax.rem(xi + d, nx) * ny + yi) * nc + core
                remote(vxy.at[xi, part], vxy.at[xi, part], 8, "ctx", peer).start()

    second_hop(0, AFTER_QUERY)

    new_k = rotated(total[16:18] * rms, 1).astype(BF16).astype(F32)
    new_v = (total[18:20] * rms).astype(BF16).astype(F32)
    qf = q_own.astype(F32)
    second = lax.broadcasted_iota(jnp.int32, (16, HEAD), 0) >= GROUP
    own_1 = jnp.sum(qf * new_k[0:1], axis=1, keepdims=True) * SCALE
    own_2 = jnp.sum(qf * new_k[1:2], axis=1, keepdims=True) * SCALE
    own_1 = jnp.broadcast_to(own_1, (16, HEAD))
    own_2 = jnp.where(second, jnp.broadcast_to(own_2, (16, HEAD)), NEGATIVE)
    own_max = jnp.maximum(own_1, own_2)
    own_w1 = jnp.exp(own_1 - own_max).astype(BF16).astype(F32)
    own_w2 = jnp.exp(own_2 - own_max).astype(BF16).astype(F32)
    own_total = own_w1 + own_w2
    own_out = own_w1 * new_v[0:1] + own_w2 * new_v[1:2]
    own_kv[0] = own_max
    own_kv[1] = own_total
    own_kv[2] = own_out

    scan[0, 0:16] = jnp.full((16, HEAD), NEGATIVE, F32)
    scan[0, 16:48] = jnp.zeros((32, HEAD), F32)
    wait_bytes(q_all.at[pl.ds(0, n - 1)], recv_sem.at[1])
    token = lax.broadcasted_iota(jnp.int32, (16, PAGE), 1)
    for s in range(cap):
        flat = jnp.maximum(tab_s[s, 0] - 1, 0)
        present = tab_s[s, 0] > 0
        owner = jnp.right_shift(flat, pages.bit_length() - 1)
        page = jnp.bitwise_and(flat, pages - 1)
        count = jnp.where(present, lengths_s[owner] - page * PAGE, 0)
        product = lax.dot_general(
            q_all[owner], kbuf[s], (((1,), (1,)), ((), ())), preferred_element_type=F32
        )
        scores[s] = jnp.where(token < count, product * SCALE, NEGATIVE)
    for s in range(cap):
        flat = jnp.maximum(tab_s[s, 0] - 1, 0)
        present = tab_s[s, 0] > 0
        owner = jnp.right_shift(flat, pages.bit_length() - 1)
        page = jnp.bitwise_and(flat, pages - 1)
        count = jnp.where(present, lengths_s[owner] - page * PAGE, 0)
        row = scores[s]
        top = jnp.max(row, axis=1, keepdims=True)
        exact = jnp.where(token < count, jnp.exp(row - top), 0.0).astype(BF16)
        weights[s] = exact
        blocks[s, 0:16] = jnp.broadcast_to(top, (16, HEAD))
        blocks[s, 16:32] = jnp.broadcast_to(
            jnp.sum(exact.astype(F32), axis=1, keepdims=True), (16, HEAD)
        )
    for s in range(cap):
        blocks[s, 32:48] = jnp.dot(weights[s], vbuf[s], preferred_element_type=F32)
    for s in range(cap):
        before = tab_s[s, 1]
        top_b, top = scan[before, 0:16], blocks[s, 0:16]
        peak = jnp.maximum(top_b, top)
        scale_b, scale = jnp.exp(top_b - peak), jnp.exp(top - peak)
        scan[s + 1, 0:16] = peak
        scan[s + 1, 16:32] = scan[before, 16:32] * scale_b + blocks[s, 16:32] * scale
        scan[s + 1, 32:48] = scan[before, 32:48] * scale_b + blocks[s, 32:48] * scale

    lane16 = lax.broadcasted_iota(jnp.int32, (16, HEAD), 1)
    row16 = lax.broadcasted_iota(jnp.int32, (16, HEAD), 0)
    for r in range(requests):
        at = tab_s[r, 2]
        send_c[r] = scan[at, 32:48].astype(BF16)
        both = jnp.where(lane16 == row16 + 16, scan[at, 16:32], 0.0)
        both = jnp.where(lane16 == row16, scan[at, 0:16], both)
        send_m[r] = jnp.sum(both, axis=0, keepdims=True)
    for peer, at in peers:
        remote(send_m.at[peer], recv_m.at[at], 10, "ctx", peer).start()
        remote(send_c.at[peer], recv_c.at[at], 2, "ctx", peer).start()
    recv_c[0] = send_c[me]
    recv_m[0] = send_m[me]
    second_hop(AFTER_QUERY, AFTER_QUERY + AFTER_BLOCKS)

    leave_0 = from_s[2 * me] - me * slots
    leave_1 = from_s[2 * me + 1] - me * slots

    for s in range(cap):
        gone = (s == leave_0) | (s == leave_1)
        kbuf[s] = jnp.where(gone, jnp.zeros((), BF16), kbuf[s])
        vbuf[s] = jnp.where(gone, jnp.zeros((), BF16), vbuf[s])

    out_k0 = pltpu.make_async_copy(kbuf.at[pl.ds(0, cap)], mk_hbm.at[pl.ds(0, cap)], out_sem.at[2])
    out_v0 = pltpu.make_async_copy(vbuf.at[pl.ds(0, cap)], mv_hbm.at[pl.ds(0, cap)], out_sem.at[3])
    out_k0.start()
    out_v0.start()

    wait_bytes(recv_m.at[pl.ds(1, n - 1)], recv_sem.at[10])
    peak = own_kv[0]
    for j in range(n):
        row = jnp.broadcast_to(recv_m[j], (16, HEAD))
        top = jnp.sum(jnp.where(lane16 == row16, row, 0.0), axis=1, keepdims=True)
        amount = jnp.sum(jnp.where(lane16 == row16 + 16, row, 0.0), axis=1, keepdims=True)
        asm[j * 32 : j * 32 + 16, :] = jnp.broadcast_to(top, (16, HEAD))
        asm[j * 32 + 16 : j * 32 + 32, :] = jnp.broadcast_to(amount, (16, HEAD))
        peak = jnp.maximum(peak, asm[j * 32 : j * 32 + 16, :])
    own_scale = jnp.exp(own_kv[0] - peak)
    denominator = own_kv[1] * own_scale
    numerator = own_kv[2] * own_scale
    for j in range(n):
        scale = jnp.exp(asm[j * 32 : j * 32 + 16, :] - peak)
        denominator = denominator + asm[j * 32 + 16 : j * 32 + 32, :] * scale
        asm[j * 32 : j * 32 + 16, :] = scale
    wait_bytes(recv_c.at[pl.ds(1, n - 1)], recv_sem.at[2])
    for j in range(n):
        numerator = numerator + recv_c[j].astype(F32) * asm[j * 32 : j * 32 + 16, :]
    att_all[me] = (numerator / denominator).astype(BF16)

    for peer, _ in peers:
        remote(att_all.at[me], att_all.at[me], 3, "ctx", peer).start()

    second_hop(AFTER_QUERY + AFTER_BLOCKS, max(nx, ny))

    loads[4].wait()
    wait_bytes(att_all.at[pl.ds(0, n - 1)], recv_sem.at[3])
    for r in range(requests):
        att_f[r * 16 : r * 16 + 16, :] = att_all[r].astype(F32)
    attention = jnp.concatenate(
        [
            jnp.concatenate(
                [att_f[pl.ds(step * GROUP + h, requests, stride=16), :] for h in range(GROUP)],
                axis=1,
            )
            for step in range(2)
        ],
        axis=0,
    ).astype(BF16)
    projected = jnp.dot(attention, wo[...], preferred_element_type=F32)
    for t in range(tsize):
        for step in range(2):
            p_send[t, step * rows_t : (step + 1) * rows_t] = projected[
                step * requests + t * rows_t : step * requests + (t + 1) * rows_t
            ]

    for j in far_first(tsize):
        peer = lax.rem(mt + j, tsize)
        remote(p_send.at[peer], p_recv.at[j], 4, "tp", peer).start()

    wait_bytes(kxy.at[pl.ds(0, ny - 1)], recv_sem.at[7])
    wait_bytes(vxy.at[pl.ds(0, nx - 1)], recv_sem.at[8])

    def source_of(mark):
        index = jnp.maximum(mark - 1, 0)
        device = jnp.right_shift(index, 1)
        which = jnp.bitwise_and(index, 1)
        src_core = lax.rem(device, nc)
        src_y = lax.rem(device // nc, ny)
        src_x = device // (nc * ny)
        return src_x, src_y, src_core, which

    for i in range(ARRIVALS):
        src_x, src_y, _, which = source_of(tab_s[i, 4])
        sib_send[0, i] = kxy[src_y, src_x, which]
        sib_send[1, i] = vxy[src_x, src_y, which]
    remote(sib_send, sib_recv, 9, "ctx", sibling).start()

    wait_bytes(sib_recv, recv_sem.at[9])
    for i in range(ARRIVALS):
        mark = tab_s[i, 3]
        src_x, src_y, src_core, which = source_of(mark)
        here = src_core == core
        arrived = mark > 0
        new_page = jnp.where(here, kxy[src_y, src_x, which], sib_recv[0, i])
        kbuf[cap + i] = jnp.where(arrived, new_page, kbuf[cap + i])
        new_page = jnp.where(here, vxy[src_x, src_y, which], sib_recv[1, i])
        vbuf[cap + i] = jnp.where(arrived, new_page, vbuf[cap + i])
    rest = pl.ds(cap, ARRIVALS)
    out_k = pltpu.make_async_copy(kbuf.at[rest], mk_hbm.at[rest], out_sem.at[0])
    out_v = pltpu.make_async_copy(vbuf.at[rest], mv_hbm.at[rest], out_sem.at[1])
    out_k.start()
    out_v.start()

    residual_1 = jnp.zeros((rows_t, x1_v.shape[1]), F32)
    residual_2 = residual_1
    x1_f, x2_f = x1_v[...].astype(F32), x2_v[...].astype(F32)
    for t in range(tsize):
        rows = slice(t * rows_t, (t + 1) * rows_t)
        residual_1 = jnp.where(mt == t, x1_f[rows], residual_1)
        residual_2 = jnp.where(mt == t, x2_f[rows], residual_2)

    wait_bytes(p_recv.at[pl.ds(1, tsize - 1)], recv_sem.at[4])
    summed = p_send[mt]
    for j in range(1, tsize):
        summed = summed + p_recv[j]
    o1_v[...] = (residual_1 + summed[:rows_t]).astype(BF16)
    o2_v[...] = (residual_2 + summed[rows_t:]).astype(BF16)

    wait_bytes(recv_a.at[pl.ds(1, n - 1)], send_sem.at[0])
    wait_bytes(q_all.at[pl.ds(0, n - 1)], send_sem.at[1])
    wait_bytes(recv_c.at[pl.ds(1, n - 1)], send_sem.at[2])
    wait_bytes(att_all.at[pl.ds(0, n - 1)], send_sem.at[3])
    wait_bytes(p_recv.at[pl.ds(1, tsize - 1)], send_sem.at[4])
    wait_bytes(kxy.at[0, pl.ds(0, nx - 1)], send_sem.at[5])
    wait_bytes(vxy.at[0, pl.ds(0, ny - 1)], send_sem.at[6])
    wait_bytes(kxy.at[pl.ds(0, ny - 1)], send_sem.at[7])
    wait_bytes(vxy.at[pl.ds(0, nx - 1)], send_sem.at[8])
    wait_bytes(sib_send, send_sem.at[9])
    wait_bytes(recv_m.at[pl.ds(1, n - 1)], send_sem.at[10])
    out_k.wait()
    out_v.wait()
    out_k0.wait()
    out_v0.wait()


def grid_of(n):
    cores = 2
    side = int(round((n // cores) ** 0.5))
    return (n // cores // side, side, cores)


def per_device(
    n,
    tsize,
    x_first,
    x_second,
    norm_gain,
    w_query,
    key_value_weight,
    w_out,
    key_cache,
    value_cache,
    lengths,
    page_table,
    move_from,
    move_to,
):
    requests, depth = x_first.shape
    slots = key_cache.shape[0]
    cap = slots - ARRIVALS
    nx, ny, nc = grid_of(n)
    rows_t = requests // tsize
    rows_n = -(-max(cap, requests) // 8) * 8
    vmem = pl.BlockSpec(memory_space=pltpu.VMEM)
    anywhere = pl.BlockSpec(memory_space=pl.ANY)
    out = pl.pallas_call(
        functools.partial(kernel, n, tsize, (nx, ny, nc), depth * n),
        out_shape=(
            jax.ShapeDtypeStruct((rows_t, depth), BF16),
            jax.ShapeDtypeStruct((rows_t, depth), BF16),
            jax.ShapeDtypeStruct(key_cache.shape, BF16),
            jax.ShapeDtypeStruct(value_cache.shape, BF16),
        ),
        in_specs=[anywhere] * 12,
        out_specs=(vmem, vmem, anywhere, anywhere),
        scratch_shapes=[
            pltpu.SMEM(lengths.shape, jnp.int32),
            pltpu.SMEM(move_from.shape, jnp.int32),
            pltpu.VMEM((1,) + move_to.shape, jnp.int32),
            pltpu.VMEM(page_table.shape, jnp.int32),
            pltpu.VMEM(x_first.shape, BF16),
            pltpu.VMEM(x_second.shape, BF16),
            pltpu.VMEM(norm_gain.shape, BF16),
            pltpu.VMEM(w_query.shape, BF16),
            pltpu.VMEM(key_value_weight.shape, BF16),
            pltpu.VMEM(w_out.shape, BF16),
            pltpu.VMEM(key_cache.shape, BF16),
            pltpu.VMEM(value_cache.shape, BF16),
            pltpu.VMEM((n * 32, HEAD), F32),
            pltpu.VMEM((n, 32, HEAD), BF16),
            pltpu.VMEM((n, 32, HEAD), BF16),
            pltpu.VMEM((n, 16, HEAD), BF16),
            pltpu.VMEM((3, 16, HEAD), F32),
            pltpu.VMEM((128, page_table.shape[1]), jnp.int32),
            pltpu.VMEM((rows_n, 128), jnp.int32),
            pltpu.SMEM((rows_n, 128), jnp.int32),
            pltpu.VMEM((cap, 16, PAGE), F32),
            pltpu.VMEM((cap, 16, PAGE), BF16),
            pltpu.VMEM((cap, 48, HEAD), F32),
            pltpu.VMEM((cap + 1, 48, HEAD), F32),
            pltpu.VMEM((n, 16, HEAD), BF16),
            pltpu.VMEM((n, 16, HEAD), BF16),
            pltpu.VMEM((n, 1, HEAD), F32),
            pltpu.VMEM((n, 1, HEAD), F32),
            pltpu.VMEM((n, 16, HEAD), BF16),
            pltpu.VMEM((n * 16, HEAD), F32),
            pltpu.VMEM((tsize, 2 * rows_t, depth), F32),
            pltpu.VMEM((tsize, 2 * rows_t, depth), F32),
            pltpu.VMEM((ny, nx, 2, PAGE, HEAD), BF16),
            pltpu.VMEM((nx, ny, 2, PAGE, HEAD), BF16),
            pltpu.VMEM((2, ARRIVALS, PAGE, HEAD), BF16),
            pltpu.VMEM((2, ARRIVALS, PAGE, HEAD), BF16),
            pltpu.SemaphoreType.DMA((12,)),
            pltpu.SemaphoreType.DMA((4,)),
            pltpu.SemaphoreType.DMA,
            pltpu.SemaphoreType.DMA((11,)),
            pltpu.SemaphoreType.DMA((11,)),
        ],
        compiler_params=pltpu.CompilerParams(
            collective_id=0, has_side_effects=True, vmem_limit_bytes=VMEM_GRANT
        ),
        name="decode_two_steps",
    )(
        lengths,
        move_from,
        move_to,
        page_table,
        x_first,
        x_second,
        norm_gain,
        w_query,
        key_value_weight,
        w_out,
        key_cache,
        value_cache,
    )
    def chunks(ref):
        size = ref.shape[0]
        step = -(-size // CHUNKS) if len(ref.shape) == 3 else size
        return [(at, min(step, size - at)) for at in range(0, size, step)]

    total = sum(len(chunks(o)) for o in out)

    def store(*refs):
        sources, targets, held = refs[:4], refs[4:8], refs[8:12]
        in_sem, out_sem = refs[12], refs[13]
        inward, outward = [], []
        for a, b, c in zip(sources, targets, held):
            for at, size in chunks(a):
                k = len(inward)
                cut = pl.ds(at, size)
                inward.append(pltpu.make_async_copy(a.at[cut], c.at[cut], in_sem.at[k]))
                outward.append(pltpu.make_async_copy(c.at[cut], b.at[cut], out_sem.at[k]))
        for copy in inward:
            copy.start()
        for first, second in zip(inward, outward):
            first.wait()
            second.start()
        for copy in outward:
            copy.wait()

    return pl.pallas_call(
        store,
        out_shape=tuple(jax.ShapeDtypeStruct(o.shape, o.dtype) for o in out),
        in_specs=[anywhere] * 4,
        out_specs=(anywhere,) * 4,
        scratch_shapes=[pltpu.VMEM(o.shape, o.dtype) for o in out]
        + [pltpu.SemaphoreType.DMA((total,))] * 2,
        compiler_params=pltpu.CompilerParams(vmem_limit_bytes=VMEM_GRANT),
        name="store_results",
    )(*out)


def solution(mesh):
    n, tsize = mesh.shape["ctx"], mesh.shape["tp"]
    in_specs = (
        P(None, "ctx"),
        P(None, "ctx"),
        P("ctx"),
        P("ctx", "tp"),
        P("ctx", "tp"),
        P("tp", "ctx"),
        P("ctx", None, "tp"),
        P("ctx", None, "tp"),
        P(),
        P(),
        P(),
        P(),
    )
    out_specs = (P("tp", "ctx"), P("tp", "ctx"), P("ctx", None, "tp"), P("ctx", None, "tp"))
    return jax.shard_map(
        functools.partial(per_device, n, tsize),
        mesh=mesh,
        in_specs=in_specs,
        out_specs=out_specs,
        check_vma=False,
    )
```

```python
import functools

import jax
import jax.numpy as jnp
import numpy as np
from jax import lax
from jax.experimental import pallas as pl
from jax.experimental.pallas import tpu as pltpu
from jax.sharding import PartitionSpec as P

HEAD = 128
GROUP = 8
PAGE = 128
ARRIVALS = 8
THETA = 500000.0
EPSILON = 1e-05
NEGATIVE = -1e30
SCALE = HEAD**-0.5
MESH = pl.DeviceIdType.MESH
F32 = jnp.float32
BF16 = jnp.bfloat16
VMEM_GRANT = 24 * 1024 * 1024

TURN_HIGH = 6.28125
TURN_MID = float(np.float32(np.round((2 * np.pi - TURN_HIGH) * 2.0**20) / 2.0**20))
TURN_LOW = float(np.float32(2 * np.pi - TURN_HIGH - TURN_MID))


def turn_reduced(angle):
    turns = jnp.floor(angle * (1.0 / (2 * np.pi)) + 0.5)
    return ((angle - turns * TURN_HIGH) - turns * TURN_MID) - turns * TURN_LOW


def split2(v):
    high = v.astype(BF16).astype(F32)
    return high, v - high


class PageRing:
    def __init__(self, held, r, c, peer_r, peer_c, send_sem, recv_sem):
        self.held, self.r, self.c = held, r, c
        self.peer_r, self.peer_c = peer_r, peer_c
        self.send_sem, self.recv_sem = send_sem, recv_sem
        self.rows, self.columns = held.shape[0], held.shape[1]
        self.sides_r = [1, -1] if self.rows == 4 else [1]
        self.sides_c = [1, -1] if self.columns == 4 else [1]
        self.near = [0] + self.sides_c
        self.far = [2] if self.columns == 4 else []
        count_r = len(self.sides_r)
        relayed = self.rows == 4
        self.blocks = [
            len(self.sides_c),
            len(self.far),
            len(self.near) * count_r,
            len(self.far) * count_r,
            len(self.near) * relayed,
            len(self.far) * relayed,
        ]

    def row(self, d):
        return lax.rem(self.r + d + self.rows, self.rows)

    def column(self, d):
        return lax.rem(self.c + d + self.columns, self.columns)

    def send(self, stage, ref, peer):
        pltpu.make_async_remote_copy(
            src_ref=ref,
            dst_ref=ref,
            send_sem=self.send_sem.at[stage],
            recv_sem=self.recv_sem.at[stage],
            device_id={"ctx": peer},
            device_id_type=MESH,
        ).start()

    def wait(self, sem, stage):
        count = self.blocks[stage]
        if not count:
            return
        wide = max(w for w in range(1, self.columns + 1) if count % w == 0)
        ref = self.held.at[pl.ds(0, count // wide), pl.ds(0, wide)]
        pltpu.make_async_copy(ref, ref, sem.at[stage]).wait()

    def arrived(self, stage):
        self.wait(self.recv_sem, stage)

    def left(self):
        for stage in range(6):
            self.wait(self.send_sem, stage)

    def first_near(self):
        for d in self.sides_c:
            self.send(0, self.held.at[self.r, self.c], self.peer_c(d))

    def first_far(self):
        self.arrived(0)
        for _ in self.far:
            for page, d in enumerate(self.sides_c):
                self.send(1, self.held.at[self.r, self.column(-d), page], self.peer_c(d))

    def second_near(self, stage, columns):
        for e in columns:
            for d in self.sides_r:
                self.send(stage, self.held.at[self.r, self.column(e)], self.peer_r(d))

    def second_far(self, stage, columns):
        if self.rows == 4:
            for e in columns:
                for page, d in enumerate(self.sides_r):
                    self.send(
                        stage, self.held.at[self.row(-d), self.column(e), page], self.peer_r(d)
                    )


def kernel(
    n,
    tsize,
    grid_xyc,
    width,
    lengths_hbm,
    from_hbm,
    to_hbm,
    table_hbm,
    x1_hbm,
    x2_hbm,
    gain_hbm,
    wq_hbm,
    wkv_hbm,
    wo_hbm,
    kc_hbm,
    vc_hbm,
    o1_v,
    o2_v,
    kbuf,
    vbuf,
    lengths_s,
    from_s,
    to_v,
    table_v,
    x1_v,
    x2_v,
    gain_v,
    wq,
    wkv,
    wo,
    asm,
    asm_kv,
    send_s,
    recv_s,
    send_kv,
    recv_kv,
    send_a,
    recv_a,
    q_all,
    slots_t,
    tab_v,
    tab_s,
    scores,
    weights,
    blocks,
    scan,
    send_c,
    recv_c,
    send_m,
    recv_m,
    att_all,
    att_f,
    p_part,
    p_send,
    p_recv,
    kxy,
    vxy,
    sib_send,
    sib_recv,
    load_sem,
    tab_sem,
    send_sem,
    recv_sem,
    page_send,
    page_recv,
):
    nx, ny, nc = grid_xyc
    me = lax.axis_index("ctx")
    mt = lax.axis_index("tp")
    core = lax.rem(me, nc)
    yi = lax.rem(me // nc, ny)
    xi = me // (nc * ny)
    requests = x1_v.shape[0]
    pages = table_v.shape[1]
    slots = kbuf.shape[0]
    cap = slots - ARRIVALS
    rows_t = requests // tsize
    depth = x1_v.shape[1]

    loads = [
        pltpu.make_async_copy(src, dst, load_sem.at[i])
        for i, (src, dst) in enumerate(
            [
                (wq_hbm, wq),
                (wkv_hbm, wkv),
                (kc_hbm, kbuf),
                (vc_hbm, vbuf),
                (wo_hbm, wo),
                (x1_hbm, x1_v),
                (x2_hbm, x2_v),
                (gain_hbm, gain_v),
                (lengths_hbm, lengths_s),
                (from_hbm, from_s),
                (to_hbm, to_v.at[0]),
                (table_hbm, table_v),
            ]
        )
    ]
    def hops(d, size):
        return min(d, size - d)

    offsets = [(a, b, c) for a in range(nx) for b in range(ny) for c in range(nc)][1:]
    offsets.sort(key=lambda o: -(hops(o[0], nx) + hops(o[1], ny)))
    peers = [
        (
            (lax.rem(xi + a, nx) * ny + lax.rem(yi + b, ny)) * nc + lax.rem(core + c, nc),
            (a * ny + b) * nc + c,
        )
        for a, b, c in offsets
    ]

    def far_first(size):
        return sorted(range(1, size), key=lambda d: -hops(d, size))

    barrier = pltpu.get_barrier_semaphore()

    for peer, _ in peers:
        pl.semaphore_signal(barrier, inc=1, device_id={"ctx": peer}, device_id_type=MESH)
    for at in (5, 6, 7, 1, 0, 2, 3, 8, 9, 10, 11, 4):
        loads[at].start()
    for j in far_first(tsize):
        pl.semaphore_signal(
            barrier, inc=1, device_id={"tp": lax.rem(mt + j, tsize)}, device_id_type=MESH
        )

    def remote(src, dst, at, axis, peer):
        return pltpu.make_async_remote_copy(
            src_ref=src,
            dst_ref=dst,
            send_sem=send_sem.at[at],
            recv_sem=recv_sem.at[at],
            device_id={axis: peer},
            device_id_type=MESH,
        )

    def wait_bytes(ref, sem):
        pltpu.make_async_copy(ref, ref, sem).wait()

    for at in (5, 6, 7):
        loads[at].wait()
    x_both = jnp.concatenate([x1_v[...], x2_v[...]], axis=0).astype(F32)
    squares = jnp.sum(x_both * x_both, axis=1, keepdims=True)
    scaled = (x_both * gain_v[...].astype(F32)[None, :]).astype(BF16)
    lane_r = lax.broadcasted_iota(jnp.int32, (requests, HEAD), 1)
    both = jnp.where(lane_r < HEAD // 2, squares[:requests], squares[requests:])
    for r in range(requests):
        send_s[r] = both[r : r + 1]
    loads[1].wait()
    kv_part = jnp.dot(scaled, wkv[...], preferred_element_type=F32)
    for step in range(2):
        rows = slice(step * requests, (step + 1) * requests)
        asm_kv[pl.ds(step, requests, stride=8), :] = kv_part[rows, :HEAD]
        asm_kv[pl.ds(2 + step, requests, stride=8), :] = kv_part[rows, HEAD:]
    loads[0].wait()
    for h in range(GROUP):
        part = jnp.dot(scaled, wq[:, h * HEAD : (h + 1) * HEAD], preferred_element_type=F32)
        for step in range(2):
            rows = slice(step * requests, (step + 1) * requests)
            asm[pl.ds(step * GROUP + h, requests, stride=16), :] = part[rows]

    for r in range(requests):
        send_a[r] = asm[r * 16 : r * 16 + 16, :].astype(BF16)
    pl.semaphore_wait(barrier, n - 1 + tsize - 1)

    for peer, at in peers:
        remote(send_s.at[peer], recv_s.at[at], 11, "ctx", peer).start()
        remote(send_a.at[peer], recv_a.at[at], 0, "ctx", peer).start()
    for r in range(requests):
        send_kv[r] = asm_kv[r * 8 : r * 8 + 4, :]

    for at in (2, 3, 8, 9, 10, 11):
        loads[at].wait()
    for i in range(2):
        leaving = jnp.clip(from_s[2 * me + i] - me * slots, 0, slots - 1)
        kxy[yi, xi, i] = kbuf[leaving]
        vxy[xi, yi, i] = vbuf[leaving]
    def peer_x(d):
        return (lax.rem(xi + d + nx, nx) * ny + yi) * nc + core

    def peer_y(d):
        return (xi * ny + lax.rem(yi + d + ny, ny)) * nc + core

    rings = [
        PageRing(kxy, yi, xi, peer_y, peer_x, page_send.at[0], page_recv.at[0]),
        PageRing(vxy, xi, yi, peer_x, peer_y, page_send.at[1], page_recv.at[1]),
    ]
    for ring in rings:
        ring.first_near()

    local_table = table_v[...] - me * slots
    code = (
        lax.broadcasted_iota(jnp.int32, (requests, pages), 0) * pages
        + lax.broadcasted_iota(jnp.int32, (requests, pages), 1)
        + 1
    )
    slots_t[...] = jnp.zeros(slots_t.shape, jnp.int32)
    for s in range(cap):
        found = jnp.where(local_table == s, code, 0)
        slots_t[s : s + 1, :] = jnp.max(found, axis=0, keepdims=True)
    by_slot = slots_t[...]
    rows_n = tab_v.shape[0]
    code_col = jnp.max(by_slot[:rows_n], axis=1, keepdims=True)
    code_row = jnp.max(by_slot.T, axis=0, keepdims=True)
    owner_col = jnp.right_shift(code_col - 1, pages.bit_length() - 1)
    owner_row = jnp.right_shift(code_row - 1, pages.bit_length() - 1)
    wide = (rows_n, 128)
    row_id = lax.broadcasted_iota(jnp.int32, wide, 0)
    lane_id = lax.broadcasted_iota(jnp.int32, wide, 1)
    earlier = (owner_col == owner_row) & (lane_id < row_id) & (code_row > 0)
    prev_col = jnp.max(jnp.where(earlier, lane_id + 1, 0), axis=1, keepdims=True)
    held = (owner_row == row_id) & (code_row > 0)
    last_col = jnp.max(jnp.where(held, lane_id + 1, 0), axis=1, keepdims=True)
    targets = to_v[...] - cap
    moves = targets.shape[1]
    move_row = lax.broadcasted_iota(jnp.int32, (rows_n, moves), 0)
    move_lane = lax.broadcasted_iota(jnp.int32, (rows_n, moves), 1)
    sibling = me + 1 - 2 * core
    arrive_col = jnp.max(
        jnp.where(targets - me * slots == move_row, move_lane + 1, 0), axis=1, keepdims=True
    )
    arrive_sib = jnp.max(
        jnp.where(targets - sibling * slots == move_row, move_lane + 1, 0), axis=1, keepdims=True
    )
    packed = jnp.zeros(wide, jnp.int32)
    for i, column in enumerate([code_col, prev_col, last_col, arrive_col, arrive_sib]):
        packed = jnp.where(lane_id == i, column, packed)
    tab_v[...] = packed
    tab_copy = pltpu.make_async_copy(tab_v, tab_s, tab_sem)
    tab_copy.start()

    position = lengths_s[me].astype(F32)
    lane = lax.broadcasted_iota(jnp.int32, (1, HEAD), 1)
    inverse = jnp.zeros((1, HEAD), F32)
    for i in range(HEAD // 2):
        rate = float(np.float32(THETA ** (-2.0 * i / HEAD)))
        inverse = jnp.where(lane % (HEAD // 2) == i, rate, inverse)
    sign = jnp.where(lane < HEAD // 2, -1.0, 1.0)
    angles = jnp.concatenate([position * inverse, (position + 1.0) * inverse], axis=0)
    angles = turn_reduced(angles)
    cosine = jnp.cos(angles)
    sine = jnp.sin(angles) * sign

    def by_step(v, count):
        return jnp.concatenate(
            [jnp.broadcast_to(v[0:1], (count, HEAD)), jnp.broadcast_to(v[1:2], (count, HEAD))],
            axis=0,
        )

    tab_copy.wait()
    square = send_s[me]
    wait_bytes(recv_s.at[pl.ds(1, n - 1)], recv_sem.at[11])
    for j in range(1, n):
        square = square + recv_s[j]
    rms = lax.rsqrt(square / width + EPSILON)
    turned = pltpu.roll(rms, HEAD // 2, 1)
    rms = jnp.concatenate(
        [jnp.where(lane < HEAD // 2, rms, turned), jnp.where(lane < HEAD // 2, turned, rms)], axis=0
    )
    cosine_16, sine_16 = by_step(cosine * rms, GROUP), by_step(sine * rms, GROUP)
    total = asm[pl.ds(pl.multiple_of(me * 16, 16), 16), :]
    wait_bytes(recv_a.at[pl.ds(1, n - 1)], recv_sem.at[0])
    for j in range(1, n):
        total = total + recv_a[j].astype(F32)
    q_own = (total * cosine_16 + pltpu.roll(total, HEAD // 2, 1) * sine_16).astype(BF16)
    q_all[me] = q_own

    for peer, _ in peers:
        remote(q_all.at[me], q_all.at[me], 1, "ctx", peer).start()

    for peer, at in peers:
        remote(send_kv.at[peer], recv_kv.at[at], 12, "ctx", peer).start()

    for ring in rings:
        ring.first_far()
    for ring in rings:
        ring.second_near(2, ring.near)

    scan[0, 0:16] = jnp.full((16, HEAD), NEGATIVE, F32)
    scan[0, 16:48] = jnp.zeros((32, HEAD), F32)
    wait_bytes(q_all.at[pl.ds(0, n - 1)], recv_sem.at[1])
    token = lax.broadcasted_iota(jnp.int32, (16, PAGE), 1)
    for s in range(cap):
        flat = jnp.maximum(tab_s[s, 0] - 1, 0)
        present = tab_s[s, 0] > 0
        owner = jnp.right_shift(flat, pages.bit_length() - 1)
        page = jnp.bitwise_and(flat, pages - 1)
        count = jnp.where(present, lengths_s[owner] - page * PAGE, 0)
        product = lax.dot_general(
            q_all[owner], kbuf[s], (((1,), (1,)), ((), ())), preferred_element_type=F32
        )
        scores[s] = jnp.where(token < count, product * SCALE, NEGATIVE)
    for s in range(cap):
        flat = jnp.maximum(tab_s[s, 0] - 1, 0)
        present = tab_s[s, 0] > 0
        owner = jnp.right_shift(flat, pages.bit_length() - 1)
        page = jnp.bitwise_and(flat, pages - 1)
        count = jnp.where(present, lengths_s[owner] - page * PAGE, 0)
        row = scores[s]
        top = jnp.max(row, axis=1, keepdims=True)
        exact = jnp.where(token < count, jnp.exp(row - top), 0.0).astype(BF16)
        weights[s] = exact
        blocks[s, 0:16] = jnp.broadcast_to(top, (16, HEAD))
        blocks[s, 16:32] = jnp.broadcast_to(
            jnp.sum(exact.astype(F32), axis=1, keepdims=True), (16, HEAD)
        )
    for s in range(cap):
        blocks[s, 32:48] = jnp.dot(weights[s], vbuf[s], preferred_element_type=F32)
    for s in range(cap):
        before = tab_s[s, 1]
        top_b, top = scan[before, 0:16], blocks[s, 0:16]
        peak = jnp.maximum(top_b, top)
        scale_b, scale = jnp.exp(top_b - peak), jnp.exp(top - peak)
        scan[s + 1, 0:16] = peak
        scan[s + 1, 16:32] = scan[before, 16:32] * scale_b + blocks[s, 16:32] * scale
        scan[s + 1, 32:48] = scan[before, 32:48] * scale_b + blocks[s, 32:48] * scale

    lane16 = lax.broadcasted_iota(jnp.int32, (16, HEAD), 1)
    row16 = lax.broadcasted_iota(jnp.int32, (16, HEAD), 0)

    def as_row(v, chosen):
        return jnp.sum(jnp.where(chosen, v, 0.0), axis=0, keepdims=True)

    for peer, at in peers + [(me, 0)]:
        source = tab_s[peer, 2]
        chosen = lane16 == row16 + at % 8 * 16
        out_c = send_c if at else recv_c
        out_m = send_m if at else recv_m
        out_c[at] = scan[source, 32:48].astype(BF16)
        out_m[at, 0:1] = as_row(scan[source, 0:16], chosen)
        out_m[at, 1:2] = as_row(scan[source, 16:32], chosen)
    for peer, at in peers:
        remote(send_m.at[at], recv_m.at[at], 10, "ctx", peer).start()
        remote(send_c.at[at], recv_c.at[at], 2, "ctx", peer).start()
    for ring in rings:
        ring.arrived(1)
        ring.second_near(3, ring.far)
    for ring in rings:
        ring.arrived(2)
        ring.second_far(4, ring.near)

    new = asm_kv[pl.ds(pl.multiple_of(me * 8, 8), 4), :]
    wait_bytes(recv_kv.at[pl.ds(1, n - 1)], recv_sem.at[12])
    for j in range(1, n):
        new = new + recv_kv[j]
    new_k = new[0:2] * rms
    new_k = (new_k * cosine + pltpu.roll(new_k, HEAD // 2, 1) * sine).astype(BF16).astype(F32)
    new_v = (new[2:4] * rms).astype(BF16).astype(F32)
    qf = q_own.astype(F32)
    own_1 = jnp.sum(qf * new_k[0:1], axis=1, keepdims=True) * SCALE
    own_2 = jnp.sum(qf * new_k[1:2], axis=1, keepdims=True) * SCALE
    own_1 = jnp.broadcast_to(own_1, (16, HEAD))
    own_2 = jnp.where(row16 >= GROUP, jnp.broadcast_to(own_2, (16, HEAD)), NEGATIVE)
    own_max = jnp.maximum(own_1, own_2)
    own_w1 = jnp.exp(own_1 - own_max).astype(BF16).astype(F32)
    own_w2 = jnp.exp(own_2 - own_max).astype(BF16).astype(F32)
    own_out = own_w1 * new_v[0:1] + own_w2 * new_v[1:2]
    repeated = lane16 % 16 == row16
    own_max_row = as_row(own_max, repeated)
    own_total_row = as_row(own_w1 + own_w2, repeated)

    leave_0 = from_s[2 * me] - me * slots
    leave_1 = from_s[2 * me + 1] - me * slots

    for s in range(cap):
        gone = (s == leave_0) | (s == leave_1)
        kbuf[s] = jnp.where(gone, jnp.zeros((), BF16), kbuf[s])
        vbuf[s] = jnp.where(gone, jnp.zeros((), BF16), vbuf[s])

    def over_groups(v, combine):
        for shift in (16, 32, 64):
            v = combine(v, pltpu.roll(v, shift, 1))
        return v

    wait_bytes(recv_m.at[pl.ds(1, n - 1)], recv_sem.at[10])
    tops, amounts = [], []
    for k in range(n // 8):
        rows = recv_m[8 * k]
        for j in range(8 * k + 1, 8 * k + 8):
            rows = rows + recv_m[j]
        tops.append(rows[0:1])
        amounts.append(rows[1:2])
    peak = over_groups(functools.reduce(jnp.maximum, tops), jnp.maximum)
    peak = jnp.maximum(peak, own_max_row)
    scales = [jnp.exp(top - peak) for top in tops]
    own_scale = jnp.exp(own_max_row - peak)
    denominator = sum(a * b for a, b in zip(amounts, scales))
    denominator = over_groups(denominator, jnp.add) + own_total_row * own_scale
    inverse_total = 1.0 / denominator
    shares = jnp.concatenate(
        [
            jnp.where(repeated, jnp.broadcast_to(scale * inverse_total, (16, HEAD)), 0.0)
            for scale in scales
        ],
        axis=1,
    )
    share_high, share_low = split2(shares)
    share_both = jnp.concatenate([share_high, share_low], axis=0).astype(BF16)
    own_share = jnp.broadcast_to(own_scale * inverse_total, (16, HEAD))
    own_share = jnp.sum(jnp.where(lane16 == row16, own_share, 0.0), axis=1, keepdims=True)
    wait_bytes(recv_c.at[pl.ds(1, n - 1)], recv_sem.at[2])
    mixed = jnp.dot(
        share_both, recv_c[...].reshape(n * 16, HEAD), preferred_element_type=F32
    )
    att_all[me] = (mixed[:16] + mixed[16:] + own_out * own_share).astype(BF16)

    for peer, _ in peers:
        remote(att_all.at[me], att_all.at[me], 3, "ctx", peer).start()

    for ring in rings:
        ring.arrived(3)
        ring.second_far(5, ring.far)

    loads[4].wait()
    wait_bytes(att_all.at[pl.ds(0, n - 1)], recv_sem.at[3])
    for r in range(requests):
        att_f[r * 16 : r * 16 + 16, :] = att_all[r].astype(F32)
    attention = jnp.concatenate(
        [
            jnp.concatenate(
                [att_f[pl.ds(step * GROUP + h, requests, stride=16), :] for h in range(GROUP)],
                axis=1,
            )
            for step in range(2)
        ],
        axis=0,
    ).astype(BF16)
    projected = jnp.dot(attention, wo[...], preferred_element_type=F32)
    wide = depth // 2
    for t in range(tsize):
        for step in range(2):
            first = step * requests + t * rows_t
            for side in range(2):
                at = side * 2 * rows_t + step * rows_t
                p_part[t, at : at + rows_t] = projected[
                    first : first + rows_t, side * wide : (side + 1) * wide
                ]
    for t in range(tsize):
        p_send[t] = p_part[t].astype(BF16)
    for j in far_first(tsize):
        peer = lax.rem(mt + j, tsize)
        remote(p_send.at[peer], p_recv.at[j], 4, "tp", peer).start()

    for ring in rings:
        ring.arrived(4)
        ring.arrived(5)

    def source_of(mark):
        index = jnp.maximum(mark - 1, 0)
        device = jnp.right_shift(index, 1)
        which = jnp.bitwise_and(index, 1)
        src_core = lax.rem(device, nc)
        src_y = lax.rem(device // nc, ny)
        src_x = device // (nc * ny)
        return src_x, src_y, src_core, which

    for i in range(ARRIVALS):
        src_x, src_y, _, which = source_of(tab_s[i, 4])
        sib_send[0, i] = kxy[src_y, src_x, which]
        sib_send[1, i] = vxy[src_x, src_y, which]
    remote(sib_send, sib_recv, 9, "ctx", sibling).start()

    wait_bytes(sib_recv, recv_sem.at[9])
    for i in range(ARRIVALS):
        mark = tab_s[i, 3]
        src_x, src_y, src_core, which = source_of(mark)
        here = src_core == core
        arrived = mark > 0
        new_page = jnp.where(here, kxy[src_y, src_x, which], sib_recv[0, i])
        kbuf[cap + i] = jnp.where(arrived, new_page, kbuf[cap + i])
        new_page = jnp.where(here, vxy[src_x, src_y, which], sib_recv[1, i])
        vbuf[cap + i] = jnp.where(arrived, new_page, vbuf[cap + i])
    residual_1 = jnp.zeros((rows_t, x1_v.shape[1]), F32)
    residual_2 = residual_1
    x1_f, x2_f = x1_v[...].astype(F32), x2_v[...].astype(F32)
    for t in range(tsize):
        rows = slice(t * rows_t, (t + 1) * rows_t)
        residual_1 = jnp.where(mt == t, x1_f[rows], residual_1)
        residual_2 = jnp.where(mt == t, x2_f[rows], residual_2)

    wait_bytes(p_recv.at[pl.ds(1, tsize - 1)], recv_sem.at[4])
    summed = p_part[mt]
    for j in range(1, tsize):
        summed = summed + p_recv[j].astype(F32)
    summed = jnp.concatenate([summed[: 2 * rows_t], summed[2 * rows_t :]], axis=1)
    o1_v[...] = (residual_1 + summed[:rows_t]).astype(BF16)
    o2_v[...] = (residual_2 + summed[rows_t:]).astype(BF16)

    wait_bytes(recv_a.at[pl.ds(1, n - 1)], send_sem.at[0])
    wait_bytes(q_all.at[pl.ds(0, n - 1)], send_sem.at[1])
    wait_bytes(recv_c.at[pl.ds(1, n - 1)], send_sem.at[2])
    wait_bytes(att_all.at[pl.ds(0, n - 1)], send_sem.at[3])
    wait_bytes(p_recv.at[pl.ds(1, tsize - 1)], send_sem.at[4])
    for ring in rings:
        ring.left()
    wait_bytes(sib_send, send_sem.at[9])
    wait_bytes(recv_m.at[pl.ds(1, n - 1)], send_sem.at[10])
    wait_bytes(recv_s.at[pl.ds(1, n - 1)], send_sem.at[11])
    wait_bytes(recv_kv.at[pl.ds(1, n - 1)], send_sem.at[12])


def grid_of(n):
    cores = 2
    side = int(round((n // cores) ** 0.5))
    return (n // cores // side, side, cores)


def per_device(
    n,
    tsize,
    x_first,
    x_second,
    norm_gain,
    w_query,
    key_value_weight,
    w_out,
    key_cache,
    value_cache,
    lengths,
    page_table,
    move_from,
    move_to,
):
    requests, depth = x_first.shape
    slots = key_cache.shape[0]
    cap = slots - ARRIVALS
    nx, ny, nc = grid_of(n)
    rows_t = requests // tsize
    rows_n = -(-max(cap, requests) // 8) * 8
    vmem = pl.BlockSpec(memory_space=pltpu.VMEM)
    anywhere = pl.BlockSpec(memory_space=pl.ANY)
    out = pl.pallas_call(
        functools.partial(kernel, n, tsize, (nx, ny, nc), depth * n),
        out_shape=(
            pltpu.VMEM((rows_t, depth), BF16),
            pltpu.VMEM((rows_t, depth), BF16),
            pltpu.VMEM(key_cache.shape, BF16),
            pltpu.VMEM(value_cache.shape, BF16),
        ),
        in_specs=[anywhere] * 12,
        out_specs=(vmem,) * 4,
        scratch_shapes=[
            pltpu.SMEM(lengths.shape, jnp.int32),
            pltpu.SMEM(move_from.shape, jnp.int32),
            pltpu.VMEM((1,) + move_to.shape, jnp.int32),
            pltpu.VMEM(page_table.shape, jnp.int32),
            pltpu.VMEM(x_first.shape, BF16),
            pltpu.VMEM(x_second.shape, BF16),
            pltpu.VMEM(norm_gain.shape, BF16),
            pltpu.VMEM(w_query.shape, BF16),
            pltpu.VMEM(key_value_weight.shape, BF16),
            pltpu.VMEM(w_out.shape, BF16),
            pltpu.VMEM((n * 16, HEAD), F32),
            pltpu.VMEM((n * 8, HEAD), F32),
            pltpu.VMEM((n, 1, HEAD), F32),
            pltpu.VMEM((n, 1, HEAD), F32),
            pltpu.VMEM((n, 4, HEAD), F32),
            pltpu.VMEM((n, 4, HEAD), F32),
            pltpu.VMEM((n, 16, HEAD), BF16),
            pltpu.VMEM((n, 16, HEAD), BF16),
            pltpu.VMEM((n, 16, HEAD), BF16),
            pltpu.VMEM((128, page_table.shape[1]), jnp.int32),
            pltpu.VMEM((rows_n, 128), jnp.int32),
            pltpu.SMEM((rows_n, 128), jnp.int32),
            pltpu.VMEM((cap, 16, PAGE), F32),
            pltpu.VMEM((cap, 16, PAGE), BF16),
            pltpu.VMEM((cap, 48, HEAD), F32),
            pltpu.VMEM((cap + 1, 48, HEAD), F32),
            pltpu.VMEM((n, 16, HEAD), BF16),
            pltpu.VMEM((n, 16, HEAD), BF16),
            pltpu.VMEM((n, 2, HEAD), F32),
            pltpu.VMEM((n, 2, HEAD), F32),
            pltpu.VMEM((n, 16, HEAD), BF16),
            pltpu.VMEM((n * 16, HEAD), F32),
            pltpu.VMEM((tsize, 4 * rows_t, depth // 2), F32),
            pltpu.VMEM((tsize, 4 * rows_t, depth // 2), BF16),
            pltpu.VMEM((tsize, 4 * rows_t, depth // 2), BF16),
            pltpu.VMEM((ny, nx, 2, PAGE, HEAD), BF16),
            pltpu.VMEM((nx, ny, 2, PAGE, HEAD), BF16),
            pltpu.VMEM((2, ARRIVALS, PAGE, HEAD), BF16),
            pltpu.VMEM((2, ARRIVALS, PAGE, HEAD), BF16),
            pltpu.SemaphoreType.DMA((12,)),
            pltpu.SemaphoreType.DMA,
            pltpu.SemaphoreType.DMA((13,)),
            pltpu.SemaphoreType.DMA((13,)),
            pltpu.SemaphoreType.DMA((2, 6)),
            pltpu.SemaphoreType.DMA((2, 6)),
        ],
        compiler_params=pltpu.CompilerParams(
            collective_id=0, has_side_effects=True, vmem_limit_bytes=VMEM_GRANT
        ),
        name="decode_two_steps",
    )(
        *(
            pltpu.with_memory_space_constraint(x, pltpu.HBM)
            for x in (
                lengths,
                move_from,
                move_to,
                page_table,
                x_first,
                x_second,
                norm_gain,
                w_query,
                key_value_weight,
                w_out,
                key_cache,
                value_cache,
            )
        )
    )

    def store(*refs):
        sem = refs[8]
        copies = [pltpu.make_async_copy(refs[i], refs[4 + i], sem.at[i]) for i in range(4)]
        for copy in copies:
            copy.start()
        for copy in copies:
            copy.wait()

    return pl.pallas_call(
        store,
        out_shape=tuple(jax.ShapeDtypeStruct(o.shape, o.dtype) for o in out),
        in_specs=[anywhere] * 4,
        out_specs=(anywhere,) * 4,
        scratch_shapes=[pltpu.SemaphoreType.DMA((4,))],
        compiler_params=pltpu.CompilerParams(vmem_limit_bytes=VMEM_GRANT),
        name="store_results",
    )(*out)


def solution(mesh):
    n, tsize = mesh.shape["ctx"], mesh.shape["tp"]
    in_specs = (
        P(None, "ctx"),
        P(None, "ctx"),
        P("ctx"),
        P("ctx", "tp"),
        P("ctx", "tp"),
        P("tp", "ctx"),
        P("ctx", None, "tp"),
        P("ctx", None, "tp"),
        P(),
        P(),
        P(),
        P(),
    )
    out_specs = (P("tp", "ctx"), P("tp", "ctx"), P("ctx", None, "tp"), P("ctx", None, "tp"))
    return jax.shard_map(
        functools.partial(per_device, n, tsize),
        mesh=mesh,
        in_specs=in_specs,
        out_specs=out_specs,
        check_vma=False,
    )
```

```python
import functools

import jax
import jax.numpy as jnp
import numpy as np
from jax import lax
from jax.experimental import pallas as pl
from jax.experimental.pallas import tpu as pltpu
from jax.sharding import PartitionSpec as P

HEAD = 128
GROUP = 8
PAGE = 128
ARRIVALS = 8
THETA = 500000.0
EPSILON = 1e-05
NEGATIVE = -1e30
SCALE = HEAD**-0.5
MESH = pl.DeviceIdType.MESH
F32 = jnp.float32
BF16 = jnp.bfloat16
VMEM_GRANT = 24 * 1024 * 1024

TURN_HIGH = 6.28125
TURN_MID = float(np.float32(np.round((2 * np.pi - TURN_HIGH) * 2.0**20) / 2.0**20))
TURN_LOW = float(np.float32(2 * np.pi - TURN_HIGH - TURN_MID))


def turn_reduced(angle):
    turns = jnp.floor(angle * (1.0 / (2 * np.pi)) + 0.5)
    return ((angle - turns * TURN_HIGH) - turns * TURN_MID) - turns * TURN_LOW


def split2(v):
    high = v.astype(BF16).astype(F32)
    return high, v - high


class PageRing:
    def __init__(self, held, r, c, peer_r, peer_c, send_sem, recv_sem):
        self.held, self.r, self.c = held, r, c
        self.peer_r, self.peer_c = peer_r, peer_c
        self.send_sem, self.recv_sem = send_sem, recv_sem
        self.rows, self.columns = held.shape[0], held.shape[1]
        self.sides_r = [1, -1] if self.rows == 4 else [1]
        self.sides_c = [1, -1] if self.columns == 4 else [1]
        self.near = [0] + self.sides_c
        self.far = [2] if self.columns == 4 else []
        count_r = len(self.sides_r)
        relayed = self.rows == 4
        self.blocks = [
            len(self.sides_c),
            len(self.far),
            len(self.near) * count_r,
            len(self.far) * count_r,
            len(self.near) * relayed,
            len(self.far) * relayed,
        ]

    def row(self, d):
        return lax.rem(self.r + d + self.rows, self.rows)

    def column(self, d):
        return lax.rem(self.c + d + self.columns, self.columns)

    def send(self, stage, ref, peer):
        pltpu.make_async_remote_copy(
            src_ref=ref,
            dst_ref=ref,
            send_sem=self.send_sem.at[stage],
            recv_sem=self.recv_sem.at[stage],
            device_id={"ctx": peer},
            device_id_type=MESH,
        ).start()

    def wait(self, sem, stage):
        count = self.blocks[stage]
        if not count:
            return
        wide = max(w for w in range(1, self.columns + 1) if count % w == 0)
        ref = self.held.at[pl.ds(0, count // wide), pl.ds(0, wide)]
        pltpu.make_async_copy(ref, ref, sem.at[stage]).wait()

    def arrived(self, stage):
        self.wait(self.recv_sem, stage)

    def left(self):
        for stage in range(6):
            self.wait(self.send_sem, stage)

    def first_near(self):
        for d in self.sides_c:
            self.send(0, self.held.at[self.r, self.c], self.peer_c(d))

    def first_far(self):
        self.arrived(0)
        for _ in self.far:
            for page, d in enumerate(self.sides_c):
                self.send(1, self.held.at[self.r, self.column(-d), page], self.peer_c(d))

    def second_near(self, stage, columns):
        for e in columns:
            for d in self.sides_r:
                self.send(stage, self.held.at[self.r, self.column(e)], self.peer_r(d))

    def second_far(self, stage, columns):
        if self.rows == 4:
            for e in columns:
                for page, d in enumerate(self.sides_r):
                    self.send(
                        stage, self.held.at[self.row(-d), self.column(e), page], self.peer_r(d)
                    )


def kernel(
    n,
    tsize,
    grid_xyc,
    width,
    lengths_hbm,
    from_hbm,
    to_hbm,
    table_hbm,
    x1_hbm,
    x2_hbm,
    gain_hbm,
    wq_hbm,
    wkv_hbm,
    wo_hbm,
    kc_hbm,
    vc_hbm,
    o1_v,
    o2_v,
    kbuf,
    vbuf,
    lengths_s,
    from_s,
    to_v,
    table_v,
    x1_v,
    x2_v,
    gain_v,
    wq,
    wkv,
    wo,
    asm,
    asm_kv,
    send_s,
    recv_s,
    send_kv,
    recv_kv,
    send_a,
    recv_a,
    q_all,
    slots_t,
    tab_v,
    tab_s,
    kt,
    valid,
    scores,
    weights,
    blocks,
    scan,
    send_c,
    recv_c,
    send_m,
    recv_m,
    att_all,
    att_f,
    p_part,
    p_send,
    p_recv,
    kxy,
    vxy,
    sib_send,
    sib_recv,
    load_sem,
    tab_sem,
    send_sem,
    recv_sem,
    page_send,
    page_recv,
):
    nx, ny, nc = grid_xyc
    me = lax.axis_index("ctx")
    mt = lax.axis_index("tp")
    core = lax.rem(me, nc)
    yi = lax.rem(me // nc, ny)
    xi = me // (nc * ny)
    requests = x1_v.shape[0]
    pages = table_v.shape[1]
    slots = kbuf.shape[0]
    cap = slots - ARRIVALS
    rows_t = requests // tsize
    depth = x1_v.shape[1]

    loads = [
        pltpu.make_async_copy(src, dst, load_sem.at[i])
        for i, (src, dst) in enumerate(
            [
                (wq_hbm, wq),
                (wkv_hbm, wkv),
                (kc_hbm, kbuf),
                (vc_hbm, vbuf),
                (wo_hbm, wo),
                (x1_hbm, x1_v),
                (x2_hbm, x2_v),
                (gain_hbm, gain_v),
                (lengths_hbm, lengths_s),
                (from_hbm, from_s),
                (to_hbm, to_v.at[0]),
                (table_hbm, table_v),
            ]
        )
    ]
    def hops(d, size):
        return min(d, size - d)

    offsets = [(a, b, c) for a in range(nx) for b in range(ny) for c in range(nc)][1:]
    offsets.sort(key=lambda o: -(hops(o[0], nx) + hops(o[1], ny)))
    peers = [
        (
            (lax.rem(xi + a, nx) * ny + lax.rem(yi + b, ny)) * nc + lax.rem(core + c, nc),
            (a * ny + b) * nc + c,
        )
        for a, b, c in offsets
    ]

    def far_first(size):
        return sorted(range(1, size), key=lambda d: -hops(d, size))

    barrier = pltpu.get_barrier_semaphore()

    for peer, _ in peers:
        pl.semaphore_signal(barrier, inc=1, device_id={"ctx": peer}, device_id_type=MESH)
    for at in (5, 6, 7, 1, 0, 2, 3, 8, 9, 10, 11, 4):
        loads[at].start()
    for j in far_first(tsize):
        pl.semaphore_signal(
            barrier, inc=1, device_id={"tp": lax.rem(mt + j, tsize)}, device_id_type=MESH
        )

    def remote(src, dst, at, axis, peer):
        return pltpu.make_async_remote_copy(
            src_ref=src,
            dst_ref=dst,
            send_sem=send_sem.at[at],
            recv_sem=recv_sem.at[at],
            device_id={axis: peer},
            device_id_type=MESH,
        )

    def wait_bytes(ref, sem):
        pltpu.make_async_copy(ref, ref, sem).wait()

    for at in (5, 6, 7):
        loads[at].wait()
    x_both = jnp.concatenate([x1_v[...], x2_v[...]], axis=0).astype(F32)
    squares = jnp.sum(x_both * x_both, axis=1, keepdims=True)
    scaled = (x_both * gain_v[...].astype(F32)[None, :]).astype(BF16)
    lane_r = lax.broadcasted_iota(jnp.int32, (requests, HEAD), 1)
    both = jnp.where(lane_r < HEAD // 2, squares[:requests], squares[requests:])
    for r in range(requests):
        send_s[r] = both[r : r + 1]
    loads[1].wait()
    kv_part = jnp.dot(scaled, wkv[...], preferred_element_type=F32)
    for step in range(2):
        rows = slice(step * requests, (step + 1) * requests)
        asm_kv[pl.ds(step, requests, stride=8), :] = kv_part[rows, :HEAD]
        asm_kv[pl.ds(2 + step, requests, stride=8), :] = kv_part[rows, HEAD:]
    loads[0].wait()
    for h in range(GROUP):
        part = jnp.dot(scaled, wq[:, h * HEAD : (h + 1) * HEAD], preferred_element_type=F32)
        for step in range(2):
            rows = slice(step * requests, (step + 1) * requests)
            asm[pl.ds(step * GROUP + h, requests, stride=16), :] = part[rows]

    for r in range(requests):
        send_a[r] = asm[r * 16 : r * 16 + 16, :].astype(BF16)
    pl.semaphore_wait(barrier, n - 1 + tsize - 1)

    for peer, at in peers:
        remote(send_s.at[peer], recv_s.at[at], 11, "ctx", peer).start()
        remote(send_a.at[peer], recv_a.at[at], 0, "ctx", peer).start()
    for r in range(requests):
        send_kv[r] = asm_kv[r * 8 : r * 8 + 4, :]

    for at in (2, 3, 8, 9, 10, 11):
        loads[at].wait()
    for i in range(2):
        leaving = jnp.clip(from_s[2 * me + i] - me * slots, 0, slots - 1)
        kxy[yi, xi, i] = kbuf[leaving]
        vxy[xi, yi, i] = vbuf[leaving]
    def peer_x(d):
        return (lax.rem(xi + d + nx, nx) * ny + yi) * nc + core

    def peer_y(d):
        return (xi * ny + lax.rem(yi + d + ny, ny)) * nc + core

    rings = [
        PageRing(kxy, yi, xi, peer_y, peer_x, page_send.at[0], page_recv.at[0]),
        PageRing(vxy, xi, yi, peer_x, peer_y, page_send.at[1], page_recv.at[1]),
    ]
    for ring in rings:
        ring.first_near()
    for ring in rings:
        ring.second_near(2, [0])

    local_table = table_v[...] - me * slots
    code = (
        lax.broadcasted_iota(jnp.int32, (requests, pages), 0) * pages
        + lax.broadcasted_iota(jnp.int32, (requests, pages), 1)
        + 1
    )
    slots_t[...] = jnp.zeros(slots_t.shape, jnp.int32)
    for s in range(cap):
        found = jnp.where(local_table == s, code, 0)
        slots_t[s : s + 1, :] = jnp.max(found, axis=0, keepdims=True)
    by_slot = slots_t[...]
    rows_n = tab_v.shape[0]
    code_col = jnp.max(by_slot[:rows_n], axis=1, keepdims=True)
    code_row = jnp.max(by_slot.T, axis=0, keepdims=True)
    owner_col = jnp.right_shift(code_col - 1, pages.bit_length() - 1)
    owner_row = jnp.right_shift(code_row - 1, pages.bit_length() - 1)
    wide = (rows_n, 128)
    row_id = lax.broadcasted_iota(jnp.int32, wide, 0)
    lane_id = lax.broadcasted_iota(jnp.int32, wide, 1)
    earlier = (owner_col == owner_row) & (lane_id < row_id) & (code_row > 0)
    prev_col = jnp.max(jnp.where(earlier, lane_id + 1, 0), axis=1, keepdims=True)
    held = (owner_row == row_id) & (code_row > 0)
    last_col = jnp.max(jnp.where(held, lane_id + 1, 0), axis=1, keepdims=True)
    targets = to_v[...] - cap
    moves = targets.shape[1]
    move_row = lax.broadcasted_iota(jnp.int32, (rows_n, moves), 0)
    move_lane = lax.broadcasted_iota(jnp.int32, (rows_n, moves), 1)
    sibling = me + 1 - 2 * core
    arrive_col = jnp.max(
        jnp.where(targets - me * slots == move_row, move_lane + 1, 0), axis=1, keepdims=True
    )
    arrive_sib = jnp.max(
        jnp.where(targets - sibling * slots == move_row, move_lane + 1, 0), axis=1, keepdims=True
    )
    packed = jnp.zeros(wide, jnp.int32)
    owner_safe = jnp.maximum(owner_col, 0)
    for i, column in enumerate(
        [code_col, prev_col, last_col, arrive_col, arrive_sib, owner_safe]
    ):
        packed = jnp.where(lane_id == i, column, packed)
    tab_v[...] = packed
    tab_copy = pltpu.make_async_copy(tab_v, tab_s, tab_sem)
    tab_copy.start()

    position = lengths_s[me].astype(F32)
    lane = lax.broadcasted_iota(jnp.int32, (1, HEAD), 1)
    inverse = jnp.zeros((1, HEAD), F32)
    for i in range(HEAD // 2):
        rate = float(np.float32(THETA ** (-2.0 * i / HEAD)))
        inverse = jnp.where(lane % (HEAD // 2) == i, rate, inverse)
    sign = jnp.where(lane < HEAD // 2, -1.0, 1.0)
    angles = jnp.concatenate([position * inverse, (position + 1.0) * inverse], axis=0)
    angles = turn_reduced(angles)
    cosine = jnp.cos(angles)
    sine = jnp.sin(angles) * sign

    def by_step(v, count):
        return jnp.concatenate(
            [jnp.broadcast_to(v[0:1], (count, HEAD)), jnp.broadcast_to(v[1:2], (count, HEAD))],
            axis=0,
        )

    tab_copy.wait()
    square = send_s[me]
    wait_bytes(recv_s.at[pl.ds(1, n - 1)], recv_sem.at[11])
    for j in range(1, n):
        square = square + recv_s[j]
    rms = lax.rsqrt(square / width + EPSILON)
    turned = pltpu.roll(rms, HEAD // 2, 1)
    rms = jnp.concatenate(
        [jnp.where(lane < HEAD // 2, rms, turned), jnp.where(lane < HEAD // 2, turned, rms)], axis=0
    )
    cosine_16, sine_16 = by_step(cosine * rms, GROUP), by_step(sine * rms, GROUP)
    total = asm[pl.ds(pl.multiple_of(me * 16, 16), 16), :]
    wait_bytes(recv_a.at[pl.ds(1, n - 1)], recv_sem.at[0])
    for j in range(1, n):
        total = total + recv_a[j].astype(F32)
    q_own = (total * cosine_16 + pltpu.roll(total, HEAD // 2, 1) * sine_16).astype(BF16)
    q_all[me] = q_own

    for peer, _ in peers:
        remote(q_all.at[me], q_all.at[me], 1, "ctx", peer).start()

    for peer, at in peers:
        remote(send_kv.at[peer], recv_kv.at[at], 12, "ctx", peer).start()

    for ring in rings:
        ring.first_far()
    for ring in rings:
        ring.second_near(2, ring.sides_c)

    scan[0, 0:16] = jnp.full((16, HEAD), NEGATIVE, F32)
    scan[0, 16:48] = jnp.zeros((32, HEAD), F32)
    token = lax.broadcasted_iota(jnp.int32, (16, PAGE), 1)
    for s in range(cap):
        kt[s] = kbuf[s].T
    for s in range(cap):
        code_s = tab_s[s, 0]
        page = jnp.bitwise_and(jnp.maximum(code_s - 1, 0), pages - 1)
        count = jnp.where(code_s > 0, lengths_s[tab_s[s, 5]] - page * PAGE, 0)
        valid[s] = jnp.where(token < count, 1.0, 0.0)
    wait_bytes(q_all.at[pl.ds(0, n - 1)], recv_sem.at[1])
    for s in range(cap):
        product = jnp.dot(q_all[tab_s[s, 5]], kt[s], preferred_element_type=F32)
        scores[s] = jnp.where(valid[s] > 0.0, product * SCALE, NEGATIVE)
    for s in range(cap):
        row = scores[s]
        top = jnp.max(row, axis=1, keepdims=True)
        exact = (jnp.exp(row - top) * valid[s]).astype(BF16)
        weights[s] = exact
        blocks[s, 0:16] = jnp.broadcast_to(top, (16, HEAD))
        blocks[s, 16:32] = jnp.broadcast_to(
            jnp.sum(exact.astype(F32), axis=1, keepdims=True), (16, HEAD)
        )
    for s in range(cap):
        blocks[s, 32:48] = jnp.dot(weights[s], vbuf[s], preferred_element_type=F32)
    for s in range(cap):
        before = tab_s[s, 1]
        top_b, top = scan[before, 0:16], blocks[s, 0:16]
        peak = jnp.maximum(top_b, top)
        scale_b, scale = jnp.exp(top_b - peak), jnp.exp(top - peak)
        scan[s + 1, 0:16] = peak
        scan[s + 1, 16:32] = scan[before, 16:32] * scale_b + blocks[s, 16:32] * scale
        scan[s + 1, 32:48] = scan[before, 32:48] * scale_b + blocks[s, 32:48] * scale

    lane16 = lax.broadcasted_iota(jnp.int32, (16, HEAD), 1)
    row16 = lax.broadcasted_iota(jnp.int32, (16, HEAD), 0)

    def as_row(v, chosen):
        return jnp.sum(jnp.where(chosen, v, 0.0), axis=0, keepdims=True)

    for peer, at in peers + [(me, 0)]:
        source = tab_s[peer, 2]
        chosen = lane16 == row16 + at % 8 * 16
        out_c = send_c if at else recv_c
        out_m = send_m if at else recv_m
        out_c[at] = scan[source, 32:48].astype(BF16)
        out_m[at, 0:1] = as_row(scan[source, 0:16], chosen)
        out_m[at, 1:2] = as_row(scan[source, 16:32], chosen)
        if at:
            remote(send_m.at[at], recv_m.at[at], 10, "ctx", peer).start()
            remote(send_c.at[at], recv_c.at[at], 2, "ctx", peer).start()
    for ring in rings:
        ring.arrived(1)
        ring.second_near(3, ring.far)
    for ring in rings:
        ring.arrived(2)
        ring.second_far(4, ring.near)

    new = asm_kv[pl.ds(pl.multiple_of(me * 8, 8), 4), :]
    wait_bytes(recv_kv.at[pl.ds(1, n - 1)], recv_sem.at[12])
    for j in range(1, n):
        new = new + recv_kv[j]
    new_k = new[0:2] * rms
    new_k = (new_k * cosine + pltpu.roll(new_k, HEAD // 2, 1) * sine).astype(BF16).astype(F32)
    new_v = (new[2:4] * rms).astype(BF16).astype(F32)
    qf = q_own.astype(F32)
    own_1 = jnp.sum(qf * new_k[0:1], axis=1, keepdims=True) * SCALE
    own_2 = jnp.sum(qf * new_k[1:2], axis=1, keepdims=True) * SCALE
    own_1 = jnp.broadcast_to(own_1, (16, HEAD))
    own_2 = jnp.where(row16 >= GROUP, jnp.broadcast_to(own_2, (16, HEAD)), NEGATIVE)
    own_max = jnp.maximum(own_1, own_2)
    own_w1 = jnp.exp(own_1 - own_max).astype(BF16).astype(F32)
    own_w2 = jnp.exp(own_2 - own_max).astype(BF16).astype(F32)
    own_out = own_w1 * new_v[0:1] + own_w2 * new_v[1:2]
    repeated = lane16 % 16 == row16
    own_max_row = as_row(own_max, repeated)
    own_total_row = as_row(own_w1 + own_w2, repeated)

    leave_0 = from_s[2 * me] - me * slots
    leave_1 = from_s[2 * me + 1] - me * slots

    for s in range(cap):
        gone = (s == leave_0) | (s == leave_1)
        kbuf[s] = jnp.where(gone, jnp.zeros((), BF16), kbuf[s])
        vbuf[s] = jnp.where(gone, jnp.zeros((), BF16), vbuf[s])

    def over_groups(v, combine):
        for shift in (16, 32, 64):
            v = combine(v, pltpu.roll(v, shift, 1))
        return v

    wait_bytes(recv_m.at[pl.ds(1, n - 1)], recv_sem.at[10])
    tops, amounts = [], []
    for k in range(n // 8):
        rows = recv_m[8 * k]
        for j in range(8 * k + 1, 8 * k + 8):
            rows = rows + recv_m[j]
        tops.append(rows[0:1])
        amounts.append(rows[1:2])
    peak = over_groups(functools.reduce(jnp.maximum, tops), jnp.maximum)
    peak = jnp.maximum(peak, own_max_row)
    scales = [jnp.exp(top - peak) for top in tops]
    own_scale = jnp.exp(own_max_row - peak)
    denominator = sum(a * b for a, b in zip(amounts, scales))
    denominator = over_groups(denominator, jnp.add) + own_total_row * own_scale
    inverse_total = 1.0 / denominator
    shares = jnp.concatenate(
        [
            jnp.where(repeated, jnp.broadcast_to(scale * inverse_total, (16, HEAD)), 0.0)
            for scale in scales
        ],
        axis=1,
    )
    share_high, share_low = split2(shares)
    share_both = jnp.concatenate([share_high, share_low], axis=0).astype(BF16)
    own_share = jnp.broadcast_to(own_scale * inverse_total, (16, HEAD))
    own_share = jnp.sum(jnp.where(lane16 == row16, own_share, 0.0), axis=1, keepdims=True)
    wait_bytes(recv_c.at[pl.ds(1, n - 1)], recv_sem.at[2])
    mixed = jnp.dot(
        share_both, recv_c[...].reshape(n * 16, HEAD), preferred_element_type=F32
    )
    att_all[me] = (mixed[:16] + mixed[16:] + own_out * own_share).astype(BF16)

    for peer, _ in peers:
        remote(att_all.at[me], att_all.at[me], 3, "ctx", peer).start()

    for ring in rings:
        ring.arrived(3)
        ring.second_far(5, ring.far)

    loads[4].wait()
    wait_bytes(att_all.at[pl.ds(0, n - 1)], recv_sem.at[3])
    for r in range(requests):
        att_f[r * 16 : r * 16 + 16, :] = att_all[r].astype(F32)
    attention = jnp.concatenate(
        [
            jnp.concatenate(
                [att_f[pl.ds(step * GROUP + h, requests, stride=16), :] for h in range(GROUP)],
                axis=1,
            )
            for step in range(2)
        ],
        axis=0,
    ).astype(BF16)
    projected = jnp.dot(attention, wo[...], preferred_element_type=F32)
    wide = depth // 2
    for t in range(tsize):
        for step in range(2):
            first = step * requests + t * rows_t
            for side in range(2):
                at = side * 2 * rows_t + step * rows_t
                p_part[t, at : at + rows_t] = projected[
                    first : first + rows_t, side * wide : (side + 1) * wide
                ]
    for t in range(tsize):
        p_send[t] = p_part[t].astype(BF16)
    for j in far_first(tsize):
        peer = lax.rem(mt + j, tsize)
        remote(p_send.at[peer], p_recv.at[j], 4, "tp", peer).start()

    for ring in rings:
        ring.arrived(4)
        ring.arrived(5)

    def source_of(mark):
        index = jnp.maximum(mark - 1, 0)
        device = jnp.right_shift(index, 1)
        which = jnp.bitwise_and(index, 1)
        src_core = lax.rem(device, nc)
        src_y = lax.rem(device // nc, ny)
        src_x = device // (nc * ny)
        return src_x, src_y, src_core, which

    for i in range(ARRIVALS):
        src_x, src_y, _, which = source_of(tab_s[i, 4])
        sib_send[0, i] = kxy[src_y, src_x, which]
        sib_send[1, i] = vxy[src_x, src_y, which]
    remote(sib_send, sib_recv, 9, "ctx", sibling).start()

    wait_bytes(sib_recv, recv_sem.at[9])
    for i in range(ARRIVALS):
        mark = tab_s[i, 3]
        src_x, src_y, src_core, which = source_of(mark)
        here = src_core == core
        arrived = mark > 0
        new_page = jnp.where(here, kxy[src_y, src_x, which], sib_recv[0, i])
        kbuf[cap + i] = jnp.where(arrived, new_page, kbuf[cap + i])
        new_page = jnp.where(here, vxy[src_x, src_y, which], sib_recv[1, i])
        vbuf[cap + i] = jnp.where(arrived, new_page, vbuf[cap + i])
    residual_1 = jnp.zeros((rows_t, x1_v.shape[1]), F32)
    residual_2 = residual_1
    x1_f, x2_f = x1_v[...].astype(F32), x2_v[...].astype(F32)
    for t in range(tsize):
        rows = slice(t * rows_t, (t + 1) * rows_t)
        residual_1 = jnp.where(mt == t, x1_f[rows], residual_1)
        residual_2 = jnp.where(mt == t, x2_f[rows], residual_2)

    wait_bytes(p_recv.at[pl.ds(1, tsize - 1)], recv_sem.at[4])
    summed = p_part[mt]
    for j in range(1, tsize):
        summed = summed + p_recv[j].astype(F32)
    summed = jnp.concatenate([summed[: 2 * rows_t], summed[2 * rows_t :]], axis=1)
    o1_v[...] = (residual_1 + summed[:rows_t]).astype(BF16)
    o2_v[...] = (residual_2 + summed[rows_t:]).astype(BF16)

    wait_bytes(recv_a.at[pl.ds(1, n - 1)], send_sem.at[0])
    wait_bytes(q_all.at[pl.ds(0, n - 1)], send_sem.at[1])
    wait_bytes(recv_c.at[pl.ds(1, n - 1)], send_sem.at[2])
    wait_bytes(att_all.at[pl.ds(0, n - 1)], send_sem.at[3])
    wait_bytes(p_recv.at[pl.ds(1, tsize - 1)], send_sem.at[4])
    for ring in rings:
        ring.left()
    wait_bytes(sib_send, send_sem.at[9])
    wait_bytes(recv_m.at[pl.ds(1, n - 1)], send_sem.at[10])
    wait_bytes(recv_s.at[pl.ds(1, n - 1)], send_sem.at[11])
    wait_bytes(recv_kv.at[pl.ds(1, n - 1)], send_sem.at[12])


def grid_of(n):
    cores = 2
    side = int(round((n // cores) ** 0.5))
    return (n // cores // side, side, cores)


def per_device(
    n,
    tsize,
    x_first,
    x_second,
    norm_gain,
    w_query,
    key_value_weight,
    w_out,
    key_cache,
    value_cache,
    lengths,
    page_table,
    move_from,
    move_to,
):
    requests, depth = x_first.shape
    slots = key_cache.shape[0]
    cap = slots - ARRIVALS
    nx, ny, nc = grid_of(n)
    rows_t = requests // tsize
    rows_n = -(-max(cap, requests) // 8) * 8
    vmem = pl.BlockSpec(memory_space=pltpu.VMEM)
    anywhere = pl.BlockSpec(memory_space=pl.ANY)
    out = pl.pallas_call(
        functools.partial(kernel, n, tsize, (nx, ny, nc), depth * n),
        out_shape=(
            pltpu.VMEM((rows_t, depth), BF16),
            pltpu.VMEM((rows_t, depth), BF16),
            pltpu.VMEM(key_cache.shape, BF16),
            pltpu.VMEM(value_cache.shape, BF16),
        ),
        in_specs=[anywhere] * 12,
        out_specs=(vmem,) * 4,
        scratch_shapes=[
            pltpu.SMEM(lengths.shape, jnp.int32),
            pltpu.SMEM(move_from.shape, jnp.int32),
            pltpu.VMEM((1,) + move_to.shape, jnp.int32),
            pltpu.VMEM(page_table.shape, jnp.int32),
            pltpu.VMEM(x_first.shape, BF16),
            pltpu.VMEM(x_second.shape, BF16),
            pltpu.VMEM(norm_gain.shape, BF16),
            pltpu.VMEM(w_query.shape, BF16),
            pltpu.VMEM(key_value_weight.shape, BF16),
            pltpu.VMEM(w_out.shape, BF16),
            pltpu.VMEM((n * 16, HEAD), F32),
            pltpu.VMEM((n * 8, HEAD), F32),
            pltpu.VMEM((n, 1, HEAD), F32),
            pltpu.VMEM((n, 1, HEAD), F32),
            pltpu.VMEM((n, 4, HEAD), F32),
            pltpu.VMEM((n, 4, HEAD), F32),
            pltpu.VMEM((n, 16, HEAD), BF16),
            pltpu.VMEM((n, 16, HEAD), BF16),
            pltpu.VMEM((n, 16, HEAD), BF16),
            pltpu.VMEM((128, page_table.shape[1]), jnp.int32),
            pltpu.VMEM((rows_n, 128), jnp.int32),
            pltpu.SMEM((rows_n, 128), jnp.int32),
            pltpu.VMEM((cap, HEAD, PAGE), BF16),
            pltpu.VMEM((cap, 16, PAGE), F32),
            pltpu.VMEM((cap, 16, PAGE), F32),
            pltpu.VMEM((cap, 16, PAGE), BF16),
            pltpu.VMEM((cap, 48, HEAD), F32),
            pltpu.VMEM((cap + 1, 48, HEAD), F32),
            pltpu.VMEM((n, 16, HEAD), BF16),
            pltpu.VMEM((n, 16, HEAD), BF16),
            pltpu.VMEM((n, 2, HEAD), F32),
            pltpu.VMEM((n, 2, HEAD), F32),
            pltpu.VMEM((n, 16, HEAD), BF16),
            pltpu.VMEM((n * 16, HEAD), F32),
            pltpu.VMEM((tsize, 4 * rows_t, depth // 2), F32),
            pltpu.VMEM((tsize, 4 * rows_t, depth // 2), BF16),
            pltpu.VMEM((tsize, 4 * rows_t, depth // 2), BF16),
            pltpu.VMEM((ny, nx, 2, PAGE, HEAD), BF16),
            pltpu.VMEM((nx, ny, 2, PAGE, HEAD), BF16),
            pltpu.VMEM((2, ARRIVALS, PAGE, HEAD), BF16),
            pltpu.VMEM((2, ARRIVALS, PAGE, HEAD), BF16),
            pltpu.SemaphoreType.DMA((12,)),
            pltpu.SemaphoreType.DMA,
            pltpu.SemaphoreType.DMA((13,)),
            pltpu.SemaphoreType.DMA((13,)),
            pltpu.SemaphoreType.DMA((2, 6)),
            pltpu.SemaphoreType.DMA((2, 6)),
        ],
        compiler_params=pltpu.CompilerParams(
            collective_id=0, has_side_effects=True, vmem_limit_bytes=VMEM_GRANT
        ),
        name="decode_two_steps",
    )(
        *(
            pltpu.with_memory_space_constraint(x, pltpu.HBM)
            for x in (
                lengths,
                move_from,
                move_to,
                page_table,
                x_first,
                x_second,
                norm_gain,
                w_query,
                key_value_weight,
                w_out,
                key_cache,
                value_cache,
            )
        )
    )

    def store(*refs):
        sem = refs[8]
        copies = [pltpu.make_async_copy(refs[i], refs[4 + i], sem.at[i]) for i in range(4)]
        for copy in copies:
            copy.start()
        for copy in copies:
            copy.wait()

    return pl.pallas_call(
        store,
        out_shape=tuple(jax.ShapeDtypeStruct(o.shape, o.dtype) for o in out),
        in_specs=[anywhere] * 4,
        out_specs=(anywhere,) * 4,
        scratch_shapes=[pltpu.SemaphoreType.DMA((4,))],
        compiler_params=pltpu.CompilerParams(vmem_limit_bytes=VMEM_GRANT),
        name="store_results",
    )(*out)


def solution(mesh):
    n, tsize = mesh.shape["ctx"], mesh.shape["tp"]
    in_specs = (
        P(None, "ctx"),
        P(None, "ctx"),
        P("ctx"),
        P("ctx", "tp"),
        P("ctx", "tp"),
        P("tp", "ctx"),
        P("ctx", None, "tp"),
        P("ctx", None, "tp"),
        P(),
        P(),
        P(),
        P(),
    )
    out_specs = (P("tp", "ctx"), P("tp", "ctx"), P("ctx", None, "tp"), P("ctx", None, "tp"))
    return jax.shard_map(
        functools.partial(per_device, n, tsize),
        mesh=mesh,
        in_specs=in_specs,
        out_specs=out_specs,
        check_vma=False,
    )
```

```python
import functools

import jax
import jax.numpy as jnp
import numpy as np
from jax import lax
from jax.experimental import pallas as pl
from jax.experimental.pallas import tpu as pltpu
from jax.sharding import PartitionSpec as P

HEAD = 128
GROUP = 8
PAGE = 128
ARRIVALS = 8
THETA = 500000.0
EPSILON = 1e-05
NEGATIVE = -1e30
SCALE = HEAD**-0.5
MESH = pl.DeviceIdType.MESH
F32 = jnp.float32
BF16 = jnp.bfloat16
VMEM_GRANT = 24 * 1024 * 1024

TURN_HIGH = 6.28125
TURN_MID = float(np.float32(np.round((2 * np.pi - TURN_HIGH) * 2.0**20) / 2.0**20))
TURN_LOW = float(np.float32(2 * np.pi - TURN_HIGH - TURN_MID))


def turn_reduced(angle):
    turns = jnp.floor(angle * (1.0 / (2 * np.pi)) + 0.5)
    return ((angle - turns * TURN_HIGH) - turns * TURN_MID) - turns * TURN_LOW


def split2(v):
    high = v.astype(BF16).astype(F32)
    return high, v - high


class PageRing:
    def __init__(self, held, r, c, peer_r, peer_c, send_sem, recv_sem):
        self.held, self.r, self.c = held, r, c
        self.peer_r, self.peer_c = peer_r, peer_c
        self.send_sem, self.recv_sem = send_sem, recv_sem
        self.rows, self.columns = held.shape[0], held.shape[1]
        self.sides_r = [1, -1] if self.rows == 4 else [1]
        self.sides_c = [1, -1] if self.columns == 4 else [1]
        self.near = [0] + self.sides_c
        self.far = [2] if self.columns == 4 else []
        count_r = len(self.sides_r)
        relayed = self.rows == 4
        self.blocks = [
            len(self.sides_c),
            len(self.far),
            len(self.near) * count_r,
            len(self.far) * count_r,
            len(self.near) * relayed,
            len(self.far) * relayed,
        ]

    def row(self, d):
        return lax.rem(self.r + d + self.rows, self.rows)

    def column(self, d):
        return lax.rem(self.c + d + self.columns, self.columns)

    def send(self, stage, ref, peer):
        pltpu.make_async_remote_copy(
            src_ref=ref,
            dst_ref=ref,
            send_sem=self.send_sem.at[stage],
            recv_sem=self.recv_sem.at[stage],
            device_id={"ctx": peer},
            device_id_type=MESH,
        ).start()

    def wait(self, sem, stage):
        count = self.blocks[stage]
        if not count:
            return
        wide = max(w for w in range(1, self.columns + 1) if count % w == 0)
        ref = self.held.at[pl.ds(0, count // wide), pl.ds(0, wide)]
        pltpu.make_async_copy(ref, ref, sem.at[stage]).wait()

    def arrived(self, stage):
        self.wait(self.recv_sem, stage)

    def left(self):
        for stage in range(6):
            self.wait(self.send_sem, stage)

    def first_near(self):
        for d in self.sides_c:
            self.send(0, self.held.at[self.r, self.c], self.peer_c(d))

    def first_far(self):
        self.arrived(0)
        for _ in self.far:
            for page, d in enumerate(self.sides_c):
                self.send(1, self.held.at[self.r, self.column(-d), page], self.peer_c(d))

    def second_near(self, stage, columns):
        for e in columns:
            for d in self.sides_r:
                self.send(stage, self.held.at[self.r, self.column(e)], self.peer_r(d))

    def second_far(self, stage, columns):
        if self.rows == 4:
            for e in columns:
                for page, d in enumerate(self.sides_r):
                    self.send(
                        stage, self.held.at[self.row(-d), self.column(e), page], self.peer_r(d)
                    )


def kernel(
    n,
    tsize,
    grid_xyc,
    width,
    lengths_hbm,
    from_hbm,
    to_hbm,
    table_hbm,
    x1_hbm,
    x2_hbm,
    gain_hbm,
    wq_hbm,
    wkv_hbm,
    wo_hbm,
    kc_hbm,
    vc_hbm,
    o1_v,
    o2_v,
    kbuf,
    vbuf,
    lengths_s,
    from_s,
    to_v,
    table_v,
    x1_v,
    x2_v,
    gain_v,
    wq,
    wkv,
    wo,
    asm,
    asm_kv,
    send_s,
    recv_s,
    send_kv,
    recv_kv,
    send_a,
    recv_a,
    q_all,
    slots_t,
    tab_v,
    tab_s,
    kt,
    valid,
    scores,
    weights,
    blocks,
    scan,
    send_c,
    recv_c,
    send_m,
    recv_m,
    att_all,
    att_f,
    p_part,
    p_send,
    p_recv,
    kxy,
    vxy,
    sib_send,
    sib_recv,
    load_sem,
    tab_sem,
    send_sem,
    recv_sem,
    page_send,
    page_recv,
):
    nx, ny, nc = grid_xyc
    me = lax.axis_index("ctx")
    mt = lax.axis_index("tp")
    core = lax.rem(me, nc)
    yi = lax.rem(me // nc, ny)
    xi = me // (nc * ny)
    requests = x1_v.shape[0]
    pages = table_v.shape[1]
    slots = kbuf.shape[0]
    cap = slots - ARRIVALS
    rows_t = requests // tsize
    depth = x1_v.shape[1]

    loads = [
        pltpu.make_async_copy(src, dst, load_sem.at[i])
        for i, (src, dst) in enumerate(
            [
                (wq_hbm, wq),
                (wkv_hbm, wkv),
                (kc_hbm, kbuf),
                (vc_hbm, vbuf),
                (wo_hbm, wo),
                (x1_hbm, x1_v),
                (x2_hbm, x2_v),
                (gain_hbm, gain_v),
                (lengths_hbm, lengths_s),
                (from_hbm, from_s),
                (to_hbm, to_v.at[0]),
                (table_hbm, table_v),
            ]
        )
    ]
    def hops(d, size):
        return min(d, size - d)

    offsets = [(a, b, c) for a in range(nx) for b in range(ny) for c in range(nc)][1:]
    offsets.sort(key=lambda o: -(hops(o[0], nx) + hops(o[1], ny)))
    peers = [
        (
            (lax.rem(xi + a, nx) * ny + lax.rem(yi + b, ny)) * nc + lax.rem(core + c, nc),
            (a * ny + b) * nc + c,
        )
        for a, b, c in offsets
    ]

    def far_first(size):
        return sorted(range(1, size), key=lambda d: -hops(d, size))

    barrier = pltpu.get_barrier_semaphore()

    for peer, _ in peers:
        pl.semaphore_signal(barrier, inc=1, device_id={"ctx": peer}, device_id_type=MESH)
    for at in (5, 6, 7, 1, 0, 2, 3, 8, 9, 10, 11, 4):
        loads[at].start()
    for j in far_first(tsize):
        pl.semaphore_signal(
            barrier, inc=1, device_id={"tp": lax.rem(mt + j, tsize)}, device_id_type=MESH
        )

    def remote(src, dst, at, axis, peer):
        return pltpu.make_async_remote_copy(
            src_ref=src,
            dst_ref=dst,
            send_sem=send_sem.at[at],
            recv_sem=recv_sem.at[at],
            device_id={axis: peer},
            device_id_type=MESH,
        )

    def wait_bytes(ref, sem):
        pltpu.make_async_copy(ref, ref, sem).wait()

    for at in (5, 6, 7):
        loads[at].wait()
    x_both = jnp.concatenate([x1_v[...], x2_v[...]], axis=0).astype(F32)
    squares = jnp.sum(x_both * x_both, axis=1, keepdims=True)
    scaled = (x_both * gain_v[...].astype(F32)[None, :]).astype(BF16)
    lane_r = lax.broadcasted_iota(jnp.int32, (requests, HEAD), 1)
    both = jnp.where(lane_r < HEAD // 2, squares[:requests], squares[requests:])
    for r in range(requests):
        send_s[r] = both[r : r + 1]
    loads[1].wait()
    kv_part = jnp.dot(scaled, wkv[...], preferred_element_type=F32)
    for step in range(2):
        rows = slice(step * requests, (step + 1) * requests)
        asm_kv[pl.ds(step, requests, stride=8), :] = kv_part[rows, :HEAD]
        asm_kv[pl.ds(2 + step, requests, stride=8), :] = kv_part[rows, HEAD:]
    loads[0].wait()
    for h in range(GROUP):
        part = jnp.dot(scaled, wq[:, h * HEAD : (h + 1) * HEAD], preferred_element_type=F32)
        for step in range(2):
            rows = slice(step * requests, (step + 1) * requests)
            asm[pl.ds(step * GROUP + h, requests, stride=16), :] = part[rows]

    for r in range(requests):
        send_a[r] = asm[r * 16 : r * 16 + 16, :].astype(BF16)
    pl.semaphore_wait(barrier, n - 1 + tsize - 1)

    for peer, at in peers:
        remote(send_s.at[peer], recv_s.at[at], 11, "ctx", peer).start()
        remote(send_a.at[peer], recv_a.at[at], 0, "ctx", peer).start()
    for r in range(requests):
        send_kv[r] = asm_kv[r * 8 : r * 8 + 4, :]

    for at in (2, 3, 8, 9, 10, 11):
        loads[at].wait()
    for i in range(2):
        leaving = jnp.clip(from_s[2 * me + i] - me * slots, 0, slots - 1)
        kxy[yi, xi, i] = kbuf[leaving]
        vxy[xi, yi, i] = vbuf[leaving]
    def peer_x(d):
        return (lax.rem(xi + d + nx, nx) * ny + yi) * nc + core

    def peer_y(d):
        return (xi * ny + lax.rem(yi + d + ny, ny)) * nc + core

    rings = [
        PageRing(kxy, yi, xi, peer_y, peer_x, page_send.at[0], page_recv.at[0]),
        PageRing(vxy, xi, yi, peer_x, peer_y, page_send.at[1], page_recv.at[1]),
    ]
    for ring in rings:
        ring.first_near()
    for ring in rings:
        ring.second_near(2, [0])

    local_table = table_v[...] - me * slots
    code = (
        lax.broadcasted_iota(jnp.int32, (requests, pages), 0) * pages
        + lax.broadcasted_iota(jnp.int32, (requests, pages), 1)
        + 1
    )
    slots_t[...] = jnp.zeros(slots_t.shape, jnp.int32)
    for s in range(cap):
        found = jnp.where(local_table == s, code, 0)
        slots_t[s : s + 1, :] = jnp.max(found, axis=0, keepdims=True)
    by_slot = slots_t[...]
    rows_n = tab_v.shape[0]
    code_col = jnp.max(by_slot[:rows_n], axis=1, keepdims=True)
    code_row = jnp.max(by_slot.T, axis=0, keepdims=True)
    owner_col = jnp.right_shift(code_col - 1, pages.bit_length() - 1)
    owner_row = jnp.right_shift(code_row - 1, pages.bit_length() - 1)
    wide = (rows_n, 128)
    row_id = lax.broadcasted_iota(jnp.int32, wide, 0)
    lane_id = lax.broadcasted_iota(jnp.int32, wide, 1)
    earlier = (owner_col == owner_row) & (lane_id < row_id) & (code_row > 0)
    prev_col = jnp.max(jnp.where(earlier, lane_id + 1, 0), axis=1, keepdims=True)
    held = (owner_row == row_id) & (code_row > 0)
    last_col = jnp.max(jnp.where(held, lane_id + 1, 0), axis=1, keepdims=True)
    targets = to_v[...] - cap
    moves = targets.shape[1]
    move_row = lax.broadcasted_iota(jnp.int32, (rows_n, moves), 0)
    move_lane = lax.broadcasted_iota(jnp.int32, (rows_n, moves), 1)
    sibling = me + 1 - 2 * core
    arrive_col = jnp.max(
        jnp.where(targets - me * slots == move_row, move_lane + 1, 0), axis=1, keepdims=True
    )
    arrive_sib = jnp.max(
        jnp.where(targets - sibling * slots == move_row, move_lane + 1, 0), axis=1, keepdims=True
    )
    packed = jnp.zeros(wide, jnp.int32)
    owner_safe = jnp.maximum(owner_col, 0)
    for i, column in enumerate(
        [code_col, prev_col, last_col, arrive_col, arrive_sib, owner_safe]
    ):
        packed = jnp.where(lane_id == i, column, packed)
    tab_v[...] = packed
    tab_copy = pltpu.make_async_copy(tab_v, tab_s, tab_sem)
    tab_copy.start()

    position = lengths_s[me].astype(F32)
    lane = lax.broadcasted_iota(jnp.int32, (1, HEAD), 1)
    inverse = jnp.zeros((1, HEAD), F32)
    for i in range(HEAD // 2):
        rate = float(np.float32(THETA ** (-2.0 * i / HEAD)))
        inverse = jnp.where(lane % (HEAD // 2) == i, rate, inverse)
    sign = jnp.where(lane < HEAD // 2, -1.0, 1.0)
    angles = jnp.concatenate([position * inverse, (position + 1.0) * inverse], axis=0)
    angles = turn_reduced(angles)
    cosine = jnp.cos(angles)
    sine = jnp.sin(angles) * sign

    def by_step(v, count):
        return jnp.concatenate(
            [jnp.broadcast_to(v[0:1], (count, HEAD)), jnp.broadcast_to(v[1:2], (count, HEAD))],
            axis=0,
        )

    tab_copy.wait()
    square = send_s[me]
    wait_bytes(recv_s.at[pl.ds(1, n - 1)], recv_sem.at[11])
    for j in range(1, n):
        square = square + recv_s[j]
    rms = lax.rsqrt(square / width + EPSILON)
    turned = pltpu.roll(rms, HEAD // 2, 1)
    rms = jnp.concatenate(
        [jnp.where(lane < HEAD // 2, rms, turned), jnp.where(lane < HEAD // 2, turned, rms)], axis=0
    )
    cosine_16, sine_16 = by_step(cosine * rms, GROUP), by_step(sine * rms, GROUP)
    total = asm[pl.ds(pl.multiple_of(me * 16, 16), 16), :]
    wait_bytes(recv_a.at[pl.ds(1, n - 1)], recv_sem.at[0])
    for j in range(1, n):
        total = total + recv_a[j].astype(F32)
    q_own = (total * cosine_16 + pltpu.roll(total, HEAD // 2, 1) * sine_16).astype(BF16)
    q_all[me] = q_own

    for peer, _ in peers:
        remote(q_all.at[me], q_all.at[me], 1, "ctx", peer).start()

    for peer, at in peers:
        remote(send_kv.at[peer], recv_kv.at[at], 12, "ctx", peer).start()

    for ring in rings:
        ring.first_far()
    for ring in rings:
        ring.second_near(2, ring.sides_c)

    scan[0, 0:16] = jnp.full((16, HEAD), NEGATIVE, F32)
    scan[0, 16:48] = jnp.zeros((32, HEAD), F32)
    token = lax.broadcasted_iota(jnp.int32, (16, PAGE), 1)
    for s in range(cap):
        kt[s] = kbuf[s].T
    for s in range(cap):
        code_s = tab_s[s, 0]
        page = jnp.bitwise_and(jnp.maximum(code_s - 1, 0), pages - 1)
        count = jnp.where(code_s > 0, lengths_s[tab_s[s, 5]] - page * PAGE, 0)
        valid[s] = jnp.where(token < count, 1.0, 0.0)
    wait_bytes(q_all.at[pl.ds(0, n - 1)], recv_sem.at[1])
    for s in range(cap):
        product = jnp.dot(q_all[tab_s[s, 5]], kt[s], preferred_element_type=F32)
        scores[s] = jnp.where(valid[s] > 0.0, product * SCALE, NEGATIVE)
    for s in range(cap):
        row = scores[s]
        top = jnp.max(row, axis=1, keepdims=True)
        exact = (jnp.exp(row - top) * valid[s]).astype(BF16)
        weights[s] = exact
        blocks[s, 0:16] = jnp.broadcast_to(top, (16, HEAD))
        blocks[s, 16:32] = jnp.broadcast_to(
            jnp.sum(exact.astype(F32), axis=1, keepdims=True), (16, HEAD)
        )
    for s in range(cap):
        blocks[s, 32:48] = jnp.dot(weights[s], vbuf[s], preferred_element_type=F32)
    for s in range(cap):
        before = tab_s[s, 1]
        top_b, top = scan[before, 0:16], blocks[s, 0:16]
        peak = jnp.maximum(top_b, top)
        scale_b, scale = jnp.exp(top_b - peak), jnp.exp(top - peak)
        scan[s + 1, 0:16] = peak
        scan[s + 1, 16:32] = scan[before, 16:32] * scale_b + blocks[s, 16:32] * scale
        scan[s + 1, 32:48] = scan[before, 32:48] * scale_b + blocks[s, 32:48] * scale

    lane16 = lax.broadcasted_iota(jnp.int32, (16, HEAD), 1)
    row16 = lax.broadcasted_iota(jnp.int32, (16, HEAD), 0)

    def as_row(v, chosen):
        return jnp.sum(jnp.where(chosen, v, 0.0), axis=0, keepdims=True)

    for peer, at in peers + [(me, 0)]:
        source = tab_s[peer, 2]
        chosen = lane16 == row16 + at % 8 * 16
        out_c = send_c if at else recv_c
        out_m = send_m if at else recv_m
        out_c[at] = scan[source, 32:48].astype(BF16)
        out_m[at, 0:1] = as_row(scan[source, 0:16], chosen)
        out_m[at, 1:2] = as_row(scan[source, 16:32], chosen)
        if at:
            remote(send_m.at[at], recv_m.at[at], 10, "ctx", peer).start()
            remote(send_c.at[at], recv_c.at[at], 2, "ctx", peer).start()
    for ring in rings:
        ring.arrived(1)
        ring.second_near(3, ring.far)
    for ring in rings:
        ring.arrived(2)
        ring.second_far(4, ring.near)

    new = asm_kv[pl.ds(pl.multiple_of(me * 8, 8), 4), :]
    wait_bytes(recv_kv.at[pl.ds(1, n - 1)], recv_sem.at[12])
    for j in range(1, n):
        new = new + recv_kv[j]
    new_k = new[0:2] * rms
    new_k = (new_k * cosine + pltpu.roll(new_k, HEAD // 2, 1) * sine).astype(BF16).astype(F32)
    new_v = (new[2:4] * rms).astype(BF16).astype(F32)
    qf = q_own.astype(F32)
    own_1 = jnp.sum(qf * new_k[0:1], axis=1, keepdims=True) * SCALE
    own_2 = jnp.sum(qf * new_k[1:2], axis=1, keepdims=True) * SCALE
    own_1 = jnp.broadcast_to(own_1, (16, HEAD))
    own_2 = jnp.where(row16 >= GROUP, jnp.broadcast_to(own_2, (16, HEAD)), NEGATIVE)
    own_max = jnp.maximum(own_1, own_2)
    own_w1 = jnp.exp(own_1 - own_max).astype(BF16).astype(F32)
    own_w2 = jnp.exp(own_2 - own_max).astype(BF16).astype(F32)
    own_out = own_w1 * new_v[0:1] + own_w2 * new_v[1:2]
    repeated = lane16 % 16 == row16
    own_max_row = as_row(own_max, repeated)
    own_total_row = as_row(own_w1 + own_w2, repeated)

    leave_0 = from_s[2 * me] - me * slots
    leave_1 = from_s[2 * me + 1] - me * slots

    for s in range(cap):
        gone = (s == leave_0) | (s == leave_1)
        kbuf[s] = jnp.where(gone, jnp.zeros((), BF16), kbuf[s])
        vbuf[s] = jnp.where(gone, jnp.zeros((), BF16), vbuf[s])

    def over_groups(v, combine):
        for shift in (16, 32, 64):
            v = combine(v, pltpu.roll(v, shift, 1))
        return v

    wait_bytes(recv_m.at[pl.ds(1, n - 1)], recv_sem.at[10])
    tops, amounts = [], []
    for k in range(n // 8):
        rows = recv_m[8 * k]
        for j in range(8 * k + 1, 8 * k + 8):
            rows = rows + recv_m[j]
        tops.append(rows[0:1])
        amounts.append(rows[1:2])
    peak = over_groups(functools.reduce(jnp.maximum, tops), jnp.maximum)
    peak = jnp.maximum(peak, own_max_row)
    scales = [jnp.exp(top - peak) for top in tops]
    own_scale = jnp.exp(own_max_row - peak)
    denominator = sum(a * b for a, b in zip(amounts, scales))
    denominator = over_groups(denominator, jnp.add) + own_total_row * own_scale
    inverse_total = 1.0 / denominator
    shares = jnp.concatenate(
        [
            jnp.where(repeated, jnp.broadcast_to(scale * inverse_total, (16, HEAD)), 0.0)
            for scale in scales
        ],
        axis=1,
    )
    share_high, share_low = split2(shares)
    share_both = jnp.concatenate([share_high, share_low], axis=0).astype(BF16)
    own_share = jnp.broadcast_to(own_scale * inverse_total, (16, HEAD))
    own_share = jnp.sum(jnp.where(lane16 == row16, own_share, 0.0), axis=1, keepdims=True)
    wait_bytes(recv_c.at[pl.ds(1, n - 1)], recv_sem.at[2])
    mixed = jnp.dot(
        share_both, recv_c[...].reshape(n * 16, HEAD), preferred_element_type=F32
    )
    att_all[me] = (mixed[:16] + mixed[16:] + own_out * own_share).astype(BF16)

    for peer, _ in peers:
        remote(att_all.at[me], att_all.at[me], 3, "ctx", peer).start()

    for ring in rings:
        ring.arrived(3)
        ring.second_far(5, ring.far)

    loads[4].wait()
    wait_bytes(att_all.at[pl.ds(0, n - 1)], recv_sem.at[3])
    for r in range(requests):
        att_f[r * 16 : r * 16 + 16, :] = att_all[r].astype(F32)
    attention = jnp.concatenate(
        [
            jnp.concatenate(
                [att_f[pl.ds(step * GROUP + h, requests, stride=16), :] for h in range(GROUP)],
                axis=1,
            )
            for step in range(2)
        ],
        axis=0,
    ).astype(BF16)
    projected = jnp.dot(attention, wo[...], preferred_element_type=F32)
    wide = depth // 2
    for t in range(tsize):
        for step in range(2):
            first = step * requests + t * rows_t
            for side in range(2):
                at = side * 2 * rows_t + step * rows_t
                p_part[t, at : at + rows_t] = projected[
                    first : first + rows_t, side * wide : (side + 1) * wide
                ]
    for t in range(tsize):
        p_send[t] = p_part[t].astype(BF16)
    for j in far_first(tsize):
        peer = lax.rem(mt + j, tsize)
        remote(p_send.at[peer], p_recv.at[j], 4, "tp", peer).start()

    for ring in rings:
        ring.arrived(4)
        ring.arrived(5)

    def source_of(mark):
        index = jnp.maximum(mark - 1, 0)
        device = jnp.right_shift(index, 1)
        which = jnp.bitwise_and(index, 1)
        src_core = lax.rem(device, nc)
        src_y = lax.rem(device // nc, ny)
        src_x = device // (nc * ny)
        return src_x, src_y, src_core, which

    for i in range(ARRIVALS):
        src_x, src_y, _, which = source_of(tab_s[i, 4])
        sib_send[0, i] = kxy[src_y, src_x, which]
        sib_send[1, i] = vxy[src_x, src_y, which]
    remote(sib_send, sib_recv, 9, "ctx", sibling).start()

    wait_bytes(sib_recv, recv_sem.at[9])
    for i in range(ARRIVALS):
        mark = tab_s[i, 3]
        src_x, src_y, src_core, which = source_of(mark)
        here = src_core == core
        arrived = mark > 0
        new_page = jnp.where(here, kxy[src_y, src_x, which], sib_recv[0, i])
        kbuf[cap + i] = jnp.where(arrived, new_page, kbuf[cap + i])
        new_page = jnp.where(here, vxy[src_x, src_y, which], sib_recv[1, i])
        vbuf[cap + i] = jnp.where(arrived, new_page, vbuf[cap + i])
    residual_1 = jnp.zeros((rows_t, x1_v.shape[1]), F32)
    residual_2 = residual_1
    x1_f, x2_f = x1_v[...].astype(F32), x2_v[...].astype(F32)
    for t in range(tsize):
        rows = slice(t * rows_t, (t + 1) * rows_t)
        residual_1 = jnp.where(mt == t, x1_f[rows], residual_1)
        residual_2 = jnp.where(mt == t, x2_f[rows], residual_2)

    wait_bytes(p_recv.at[pl.ds(1, tsize - 1)], recv_sem.at[4])
    summed = p_part[mt]
    for j in range(1, tsize):
        summed = summed + p_recv[j].astype(F32)
    summed = jnp.concatenate([summed[: 2 * rows_t], summed[2 * rows_t :]], axis=1)
    o1_v[...] = (residual_1 + summed[:rows_t]).astype(BF16)
    o2_v[...] = (residual_2 + summed[rows_t:]).astype(BF16)

    wait_bytes(recv_a.at[pl.ds(1, n - 1)], send_sem.at[0])
    wait_bytes(q_all.at[pl.ds(0, n - 1)], send_sem.at[1])
    wait_bytes(recv_c.at[pl.ds(1, n - 1)], send_sem.at[2])
    wait_bytes(att_all.at[pl.ds(0, n - 1)], send_sem.at[3])
    wait_bytes(p_recv.at[pl.ds(1, tsize - 1)], send_sem.at[4])
    for ring in rings:
        ring.left()
    wait_bytes(sib_send, send_sem.at[9])
    wait_bytes(recv_m.at[pl.ds(1, n - 1)], send_sem.at[10])
    wait_bytes(recv_s.at[pl.ds(1, n - 1)], send_sem.at[11])
    wait_bytes(recv_kv.at[pl.ds(1, n - 1)], send_sem.at[12])


def grid_of(n):
    cores = 2
    side = int(round((n // cores) ** 0.5))
    return (n // cores // side, side, cores)


def per_device(
    n,
    tsize,
    x_first,
    x_second,
    norm_gain,
    w_query,
    key_value_weight,
    w_out,
    key_cache,
    value_cache,
    lengths,
    page_table,
    move_from,
    move_to,
):
    requests, depth = x_first.shape
    slots = key_cache.shape[0]
    cap = slots - ARRIVALS
    nx, ny, nc = grid_of(n)
    rows_t = requests // tsize
    rows_n = -(-max(cap, requests) // 8) * 8
    vmem = pl.BlockSpec(memory_space=pltpu.VMEM)
    anywhere = pl.BlockSpec(memory_space=pl.ANY)
    out = pl.pallas_call(
        functools.partial(kernel, n, tsize, (nx, ny, nc), depth * n),
        out_shape=(
            pltpu.VMEM((rows_t, depth), BF16),
            pltpu.VMEM((rows_t, depth), BF16),
            pltpu.VMEM(key_cache.shape, BF16),
            pltpu.VMEM(value_cache.shape, BF16),
        ),
        in_specs=[anywhere] * 12,
        out_specs=(vmem,) * 4,
        scratch_shapes=[
            pltpu.SMEM(lengths.shape, jnp.int32),
            pltpu.SMEM(move_from.shape, jnp.int32),
            pltpu.VMEM((1,) + move_to.shape, jnp.int32),
            pltpu.VMEM(page_table.shape, jnp.int32),
            pltpu.VMEM(x_first.shape, BF16),
            pltpu.VMEM(x_second.shape, BF16),
            pltpu.VMEM(norm_gain.shape, BF16),
            pltpu.VMEM(w_query.shape, BF16),
            pltpu.VMEM(key_value_weight.shape, BF16),
            pltpu.VMEM(w_out.shape, BF16),
            pltpu.VMEM((n * 16 + 16, HEAD), F32),
            pltpu.VMEM((n * 8 + 8, HEAD), F32),
            pltpu.VMEM((n, 1, HEAD), F32),
            pltpu.VMEM((n, 1, HEAD), F32),
            pltpu.VMEM((n, 4, HEAD), F32),
            pltpu.VMEM((n, 4, HEAD), F32),
            pltpu.VMEM((n, 16, HEAD), BF16),
            pltpu.VMEM((n, 16, HEAD), BF16),
            pltpu.VMEM((n, 16, HEAD), BF16),
            pltpu.VMEM((128, page_table.shape[1]), jnp.int32),
            pltpu.VMEM((rows_n, 128), jnp.int32),
            pltpu.SMEM((rows_n, 128), jnp.int32),
            pltpu.VMEM((cap, HEAD, PAGE), BF16),
            pltpu.VMEM((cap, 16, PAGE), F32),
            pltpu.VMEM((cap, 16, PAGE), F32),
            pltpu.VMEM((cap, 16, PAGE), BF16),
            pltpu.VMEM((cap, 48, HEAD), F32),
            pltpu.VMEM((cap + 1, 48, HEAD), F32),
            pltpu.VMEM((n, 16, HEAD), BF16),
            pltpu.VMEM((n, 16, HEAD), BF16),
            pltpu.VMEM((n, 2, HEAD), F32),
            pltpu.VMEM((n, 2, HEAD), F32),
            pltpu.VMEM((n, 16, HEAD), BF16),
            pltpu.VMEM((n * 16 + 16, HEAD), F32),
            pltpu.VMEM((tsize, 4 * rows_t, depth // 2), F32),
            pltpu.VMEM((tsize, 4 * rows_t, depth // 2), BF16),
            pltpu.VMEM((tsize, 4 * rows_t, depth // 2), BF16),
            pltpu.VMEM((ny, nx, 2, PAGE, HEAD), BF16),
            pltpu.VMEM((nx, ny, 2, PAGE, HEAD), BF16),
            pltpu.VMEM((2, ARRIVALS, PAGE, HEAD), BF16),
            pltpu.VMEM((2, ARRIVALS, PAGE, HEAD), BF16),
            pltpu.SemaphoreType.DMA((12,)),
            pltpu.SemaphoreType.DMA,
            pltpu.SemaphoreType.DMA((13,)),
            pltpu.SemaphoreType.DMA((13,)),
            pltpu.SemaphoreType.DMA((2, 6)),
            pltpu.SemaphoreType.DMA((2, 6)),
        ],
        compiler_params=pltpu.CompilerParams(
            collective_id=0, has_side_effects=True, vmem_limit_bytes=VMEM_GRANT
        ),
        name="decode_two_steps",
    )(
        *(
            pltpu.with_memory_space_constraint(x, pltpu.HBM)
            for x in (
                lengths,
                move_from,
                move_to,
                page_table,
                x_first,
                x_second,
                norm_gain,
                w_query,
                key_value_weight,
                w_out,
                key_cache,
                value_cache,
            )
        )
    )

    def store(*refs):
        sem = refs[8]
        copies = [pltpu.make_async_copy(refs[i], refs[4 + i], sem.at[i]) for i in range(4)]
        for copy in copies:
            copy.start()
        for copy in copies:
            copy.wait()

    return pl.pallas_call(
        store,
        out_shape=tuple(jax.ShapeDtypeStruct(o.shape, o.dtype) for o in out),
        in_specs=[anywhere] * 4,
        out_specs=(anywhere,) * 4,
        scratch_shapes=[pltpu.SemaphoreType.DMA((4,))],
        compiler_params=pltpu.CompilerParams(vmem_limit_bytes=VMEM_GRANT),
        name="store_results",
    )(*out)


def solution(mesh):
    n, tsize = mesh.shape["ctx"], mesh.shape["tp"]
    in_specs = (
        P(None, "ctx"),
        P(None, "ctx"),
        P("ctx"),
        P("ctx", "tp"),
        P("ctx", "tp"),
        P("tp", "ctx"),
        P("ctx", None, "tp"),
        P("ctx", None, "tp"),
        P(),
        P(),
        P(),
        P(),
    )
    out_specs = (P("tp", "ctx"), P("tp", "ctx"), P("ctx", None, "tp"), P("ctx", None, "tp"))
    return jax.shard_map(
        functools.partial(per_device, n, tsize),
        mesh=mesh,
        in_specs=in_specs,
        out_specs=out_specs,
        check_vma=False,
    )
```
